32 devices in a mesh: rep: 16 (over z, y, core), fsdp: 2 (over x).
Axes of the slice: x: 2, y: 2, z: 4, core: 2. Of those that a mesh axis runs over, the one named last changes fastest.
Arguments:
- frames: float32 [32, 1024, 1280], P('rep', 'fsdp'), may hold values from -6 to 6
- cotangent: float32 [32, 1024, 1280], P('rep', 'fsdp'), may hold values from -6 to 6
- clip_lengths: int32 [32], replicated, may hold values from 256 to 1024, as said below
- clip_slots: int32 [32], P('rep'), may hold values from 0 to 31, as said below
- gain_attn: bfloat16 [1280], P('fsdp'), may hold values from 0.25 to 1.75
- shift_attn: bfloat16 [1280], P('fsdp'), may hold values from -1.75 to 1.75
- w_qkv: bfloat16 [1280, 3840], P('fsdp'), may hold values from -0.25 to 0.25
- bias_query: bfloat16 [1280], P('fsdp'), may hold values from -3 to 3
- bias_value: bfloat16 [1280], P('fsdp'), may hold values from -3 to 3
- w_out: bfloat16 [1280, 1280], P('fsdp'), may hold values from -1 to 1
- bias_out: bfloat16 [1280], P('fsdp'), may hold values from -1.75 to 1.75
- gain_ffn: bfloat16 [1280], P('fsdp'), may hold values from 0.25 to 1.75
- shift_ffn: bfloat16 [1280], P('fsdp'), may hold values from -1.75 to 1.75
- w_up: bfloat16 [1280, 5120], P('fsdp'), may hold values from -0.15625 to 0.15625
- bias_up: bfloat16 [5120], P('fsdp'), may hold values from -3 to 3
- w_down: bfloat16 [5120, 1280], P('fsdp'), may hold values from -0.078125 to 0.078125
- bias_down: bfloat16 [1280], P('fsdp'), may hold values from -1.75 to 1.75
Outputs:
- output: float32 [32, 1024, 1280], P('rep', 'fsdp')
- frames_grad: float32 [32, 1024, 1280], P('rep', 'fsdp')
- gain_attn_grad: float32 [1280], P('fsdp')
- shift_attn_grad: float32 [1280], P('fsdp')
- w_qkv_grad: float32 [1280, 3840], P('fsdp')
- bias_query_grad: float32 [1280], P('fsdp')
- bias_value_grad: float32 [1280], P('fsdp')
- w_out_grad: float32 [1280, 1280], P('fsdp')
- bias_out_grad: float32 [1280], P('fsdp')
- gain_ffn_grad: float32 [1280], P('fsdp')
- shift_ffn_grad: float32 [1280], P('fsdp')
- w_up_grad: float32 [1280, 5120], P('fsdp')
- bias_up_grad: float32 [5120], P('fsdp')
- w_down_grad: float32 [5120, 1280], P('fsdp')
- bias_down_grad: float32 [1280], P('fsdp')
The draws below stay inside these ranges and needn't reach their ends.
Inputs may be any that keep to these rules, and one draw needn't show every extreme that they name: `clip_lengths`: every clip numbered below 16 is longer than 512 frames; clip 0 has 1024 frames and clip 16 has 256. `clip_slots`: A permutation of the clip numbers; the 2 slots of each group hold exactly one clip numbered below 16.
All inputs are finite; a program needn't handle non-finite values.
Results may differ from the reference program's by a relative error of at most 0.012.
The reference program's roundings to bfloat16 on the way count: a program that leaves them out, or rounds other values in their place, can miss the bound.
Values may be sent and summed in bfloat16 or wider, within the bound.
No kernel may reach another device: no remote copies, remote signals or barrier semaphores. Data moves between devices by JAX's collectives and lax.ppermute only.
A program may use at most 512 MiB of HBM per device.

```python
import jax
import jax.numpy as jnp
from jax import lax

D = 1280
HEADS = 16
HD = 80
FF = 5120
SEQ = 1024
MB = 2
GROUPS = 16
CLIPS = 32
FR_DEV = 512


def draw_clip_lengths(key, part):
    key = jax.random.fold_in(key, 11)
    first, second = jax.random.split(key)
    longer = jax.random.randint(first, (GROUPS,), SEQ - FR_DEV + 1, SEQ + 1)
    shorter = jax.random.randint(second, (CLIPS - GROUPS,), SEQ // 4, SEQ + 1)
    longer = longer.at[0].set(SEQ)
    shorter = shorter.at[0].set(SEQ // 4)
    return jnp.concatenate([longer, shorter]).astype(jnp.int32)


def draw_clip_slots(key, part):
    key = jax.random.fold_in(key, 23)
    first, second, third = jax.random.split(key, 3)
    longer = jax.random.permutation(first, GROUPS).astype(jnp.int32)
    shorter = jax.random.permutation(second, CLIPS - GROUPS).astype(jnp.int32) + GROUPS
    table = jnp.concatenate([longer[:, None], shorter.reshape(GROUPS, MB - 1)], axis=1)
    turned = jax.random.randint(third, (GROUPS, 1), 0, MB)
    column = (jnp.arange(MB, dtype=jnp.int32)[None, :] + turned) % MB
    return jnp.take_along_axis(table, column, axis=1).reshape(CLIPS).astype(jnp.int32)


def block_scale(own_key, shape, shards, low, largest):
    loudness = 1.0
    for axis_at, parts in shards:
        draws = jax.random.uniform(jax.random.fold_in(jax.random.fold_in(own_key, 6), axis_at), (parts,), jnp.float32, low / len(shards), largest / len(shards))
        loudness = loudness * jnp.repeat(jnp.exp(draws), shape[axis_at] // parts).reshape((-1,) + (1,) * (len(shape) - 1 - axis_at))
    return loudness


def normal_values(own_key, shape, scale, most, cuts=(), held_as=jnp.bfloat16):
    array = scale * jax.random.normal(own_key, shape, jnp.float32)
    if cuts:
        array = array * block_scale(own_key, shape, cuts, -0.22, 0.18)
    return jnp.clip(array, -most, most).astype(held_as)


def setup_inputs(seed: int = 0) -> dict:
    keys = jax.random.split(jax.random.key(seed), 18)
    frames = normal_values(keys[0], (CLIPS, SEQ, D), 1.0, 6.0, ((0, 16), (1, 2)), jnp.float32)
    cotangent = normal_values(keys[1], (CLIPS, SEQ, D), 1.0, 6.0, ((0, 16), (1, 2)), jnp.float32)
    clip_lengths = draw_clip_lengths(jax.random.fold_in(keys[17], 71), 0)
    clip_slots = draw_clip_slots(jax.random.fold_in(keys[17], 71), 0)
    gain_attn = jnp.clip(1.0 + 0.15 * jax.random.normal(keys[4], (D,), jnp.float32), 0.25, 1.75).astype(jnp.bfloat16)
    shift_attn = normal_values(keys[5], (D,), 0.3, 1.75, ((0, 2),))
    w_qkv = normal_values(keys[6], (D, 3 * D), (D // 2) ** -0.5, 0.25, ((0, 2),))
    bias_query = normal_values(keys[7], (D,), 0.5, 3.0, ((0, 2),))
    bias_value = normal_values(keys[8], (D,), 0.5, 3.0, ((0, 2),))
    w_out = normal_values(keys[9], (D, D), (D // 32) ** -0.5, 1.0, ((0, 2),))
    bias_out = normal_values(keys[10], (D,), 0.3, 1.75, ((0, 2),))
    gain_ffn = jnp.clip(1.0 + 0.15 * jax.random.normal(keys[11], (D,), jnp.float32), 0.25, 1.75).astype(jnp.bfloat16)
    shift_ffn = normal_values(keys[12], (D,), 0.3, 1.75, ((0, 2),))
    w_up = normal_values(keys[13], (D, FF), D ** -0.5, 0.15625, ((0, 2),))
    bias_up = normal_values(keys[14], (FF,), 0.5, 3.0, ((0, 2),))
    w_down = normal_values(keys[15], (FF, D), FF ** -0.5, 0.078125, ((0, 2),))
    bias_down = normal_values(keys[16], (D,), 0.3, 1.75, ((0, 2),))
    return {"frames": frames, "cotangent": cotangent, "clip_lengths": clip_lengths, "clip_slots": clip_slots, "gain_attn": gain_attn, "shift_attn": shift_attn, "w_qkv": w_qkv, "bias_query": bias_query, "bias_value": bias_value, "w_out": w_out, "bias_out": bias_out, "gain_ffn": gain_ffn, "shift_ffn": shift_ffn, "w_up": w_up, "bias_up": bias_up, "w_down": w_down, "bias_down": bias_down}


@jax.custom_vjp
def low(v):
    return lax.optimization_barrier(v.astype(jnp.bfloat16)).astype(jnp.float32)

@jax.custom_vjp
def low_back(v):
    return v

def low_keep(v):
    return (low(v), None)

def low_pass(kept, grad):
    return (grad,)

def back_keep(v):
    return (v, None)

def back_low(kept, grad):
    return (low(grad),)
low.defvjp(low_keep, low_pass)
low_back.defvjp(back_keep, back_low)

def layer_norm(rows, gain, shift):
    mean = lax.optimization_barrier(jnp.mean(rows, axis=-1, keepdims=True))
    centred = rows - mean
    spread = lax.optimization_barrier(jnp.mean(centred * centred, axis=-1, keepdims=True))
    return centred * lax.rsqrt(spread + 1e-05) * gain + shift

def clip_forward(frame_rows, length, params):
    gain_attn, shift_attn, w_qkv, bias_query, bias_value, w_out, bias_out, gain_ffn, shift_ffn, w_up, bias_up, w_down, bias_down = params
    high = lax.Precision.HIGHEST
    norm_a = low(layer_norm(frame_rows, gain_attn, shift_attn))
    qkv = jnp.dot(norm_a, w_qkv, precision=high)
    query = low_back(low(qkv[:, :D] + bias_query)).reshape(SEQ, HEADS, HD)
    key = low_back(low(qkv[:, D:2 * D])).reshape(SEQ, HEADS, HD)
    value = low_back(low(qkv[:, 2 * D:] + bias_value)).reshape(SEQ, HEADS, HD)
    scores = low_back(jnp.einsum('qhd,khd->hqk', query, key, precision=high) * HD ** (-0.5))
    valid = jnp.arange(SEQ) < length
    scores = jnp.where(valid[None, None, :], scores, -1e+30)
    probs = low(jax.nn.softmax(scores, axis=-1))
    mixed = jnp.einsum('hqk,khd->qhd', probs, value, precision=high).reshape(SEQ, D)
    attn_in = low_back(low(mixed))
    resid = frame_rows + low_back(jnp.dot(attn_in, w_out, precision=high) + bias_out)
    norm_f = low(layer_norm(resid, gain_ffn, shift_ffn))
    upward = low_back(jnp.dot(norm_f, w_up, precision=high) + bias_up)
    hidden = low(jax.nn.gelu(upward, approximate=False))
    return resid + low_back(jnp.dot(hidden, w_down, precision=high) + bias_down)

def reference(frames, cotangent, clip_lengths, clip_slots, gain_attn, shift_attn, w_qkv, bias_query, bias_value, w_out, bias_out, gain_ffn, shift_ffn, w_up, bias_up, w_down, bias_down):
    spans = clip_lengths[clip_slots]
    params = tuple((p.astype(jnp.float32) for p in (gain_attn, shift_attn, w_qkv, bias_query, bias_value, w_out, bias_out, gain_ffn, shift_ffn, w_up, bias_up, w_down, bias_down)))
    checked = jax.checkpoint(clip_forward)

    def whole(frame_all, weights):

        def advance(carry, item):
            return (carry, checked(item[0], item[1], weights))
        unused, result = lax.scan(advance, jnp.zeros((), jnp.float32), (frame_all, spans))
        return result
    output, pullback = jax.vjp(whole, frames, params)
    frames_grad, grads = pullback(cotangent)
    return (output, frames_grad) + tuple(grads)
```

```python
import functools

import jax
import jax.numpy as jnp
from jax import lax
from jax.experimental import pallas as pl
from jax.experimental.pallas import tpu as pltpu
from jax.sharding import PartitionSpec as P

HEADS = 16


def layer_norm(rows, gain, shift):
    mean = jnp.mean(rows, axis=-1, keepdims=True)
    centred = rows - mean
    spread = jnp.mean(centred * centred, axis=-1, keepdims=True)
    return centred * lax.rsqrt(spread + 1e-05) * gain + shift


def exact_gelu(values):
    return jax.nn.gelu(values, approximate=False)


def product(left, right):
    return jnp.dot(left, right, preferred_element_type=jnp.float32)


def product_left(left, right):
    return lax.dot_general(
        left, right, (((0,), (0,)), ((), ())), preferred_element_type=jnp.float32
    )


def product_right(left, right):
    return lax.dot_general(
        left, right, (((1,), (1,)), ((), ())), preferred_element_type=jnp.float32
    )


def head_blocks(query, keys, values, block):
    rows, width = query.shape
    half = width // 2
    per = HEADS // 2
    size = width // HEADS
    lower = block * half
    query_part = query[:, lower : lower + half].reshape(rows, per, size)
    key_part = keys[:, lower : lower + half].reshape(keys.shape[0], per, size)
    value_part = values[:, lower : lower + half].reshape(values.shape[0], per, size)
    return (query_part, key_part, value_part)


def masked_scores(query_part, key_part, valid, scale):
    scores = (
        jnp.einsum("qhd,khd->hqk", query_part, key_part, preferred_element_type=jnp.float32) * scale
    )
    return jnp.where(valid[None, None, :], scores, -1e30)


def attend(query, keys, values, valid):
    rows, width = query.shape
    scale = (width // HEADS) ** (-0.5)
    pieces = []
    totals = []
    for block in range(2):
        query_part, key_part, value_part = head_blocks(query, keys, values, block)
        scores = masked_scores(query_part, key_part, valid, scale)
        peak = jnp.max(scores, axis=-1, keepdims=True)
        raised = jnp.exp(scores - peak)
        summed = jnp.sum(raised, axis=-1, keepdims=True)
        probs = (raised / summed).astype(jnp.bfloat16)
        mixed = jnp.einsum("hqk,khd->qhd", probs, value_part, preferred_element_type=jnp.float32)
        pieces.append(mixed.reshape(rows, width // 2))
        totals.append(peak + jnp.log(summed))
    return (jnp.concatenate(pieces, axis=1), totals)


def attend_back(query, keys, values, valid, totals, d_mixed):
    rows, width = query.shape
    scale = (width // HEADS) ** (-0.5)
    query_grads = []
    key_grads = []
    value_grads = []
    for block in range(2):
        query_part, key_part, value_part = head_blocks(query, keys, values, block)
        upper = d_mixed[:, block * (width // 2) : (block + 1) * (width // 2)].reshape(
            query_part.shape
        )
        scores = masked_scores(query_part, key_part, valid, scale)
        probs = jnp.exp(scores - totals[block])
        d_probs = jnp.einsum("qhd,khd->hqk", upper, value_part, preferred_element_type=jnp.float32)
        centre = jnp.sum(probs * d_probs, axis=-1, keepdims=True)
        d_scores = (probs * (d_probs - centre)).astype(jnp.bfloat16)
        d_query = (
            jnp.einsum("hqk,khd->qhd", d_scores, key_part, preferred_element_type=jnp.float32)
            * scale
        )
        d_key = (
            jnp.einsum("hqk,qhd->khd", d_scores, query_part, preferred_element_type=jnp.float32)
            * scale
        )
        d_value = jnp.einsum(
            "hqk,qhd->khd", probs.astype(jnp.bfloat16), upper, preferred_element_type=jnp.float32
        )
        query_grads.append(d_query.reshape(rows, width // 2))
        key_grads.append(d_key.reshape(keys.shape[0], width // 2))
        value_grads.append(d_value.reshape(keys.shape[0], width // 2))
    return (
        jnp.concatenate(query_grads, axis=1),
        jnp.concatenate(key_grads, axis=1),
        jnp.concatenate(value_grads, axis=1),
    )


def add_tuples(first, second):
    if first is None:
        return second
    return tuple((left + right for left, right in zip(first, second)))


def weight_grads(pieces, smalls):
    norm_a, d_qkv, attn_in, d_attn, norm_f, d_up, hidden, d_out = pieces
    gain_one, shift_one, gain_two, shift_two = smalls
    width = norm_a.shape[1]
    grad_qkv = product_left(norm_a, d_qkv)
    columns = jnp.sum(d_qkv.astype(jnp.float32), axis=0)
    grad_query_bias = columns[:width]
    grad_value_bias = columns[2 * width :]
    grad_out = product_left(attn_in, d_attn)
    grad_out_bias = jnp.sum(d_attn.astype(jnp.float32), axis=0)
    grad_up = product_left(norm_f, d_up)
    grad_up_bias = jnp.sum(d_up.astype(jnp.float32), axis=0)
    grad_down = product_left(hidden, d_out)
    grad_down_bias = jnp.sum(d_out.astype(jnp.float32), axis=0)
    return (
        gain_one,
        shift_one,
        grad_qkv,
        grad_query_bias,
        grad_value_bias,
        grad_out,
        grad_out_bias,
        gain_two,
        shift_two,
        grad_up,
        grad_up_bias,
        grad_down,
        grad_down_bias,
    )


def general_device(
    frames,
    cotangent,
    clip_lengths,
    clip_slots,
    gain_attn,
    shift_attn,
    w_qkv,
    bias_query,
    bias_value,
    w_out,
    bias_out,
    gain_ffn,
    shift_ffn,
    w_up,
    bias_up,
    w_down,
    bias_down,
):
    shards = (
        gain_attn,
        shift_attn,
        w_qkv,
        bias_query,
        bias_value,
        w_out,
        bias_out,
        gain_ffn,
        shift_ffn,
        w_up,
        bias_up,
        w_down,
        bias_down,
    )
    micro, rows, width = frames.shape
    group_size = lax.axis_size("fsdp")
    length_all = rows * group_size
    positions = jnp.arange(length_all, dtype=jnp.int32)
    numbers = jnp.arange(clip_lengths.shape[0], dtype=jnp.int32)
    outputs = []
    input_grads = []
    summed = None
    kept_pieces = []
    small_sum = None
    for slot in range(micro):
        span = jnp.sum(jnp.where(numbers == clip_slots[slot], clip_lengths, 0))
        valid = positions < span
        whole = (
            lax.all_gather(shards[0], "fsdp", axis=0, tiled=True),
            lax.all_gather(shards[1], "fsdp", axis=0, tiled=True),
            lax.all_gather(shards[2], "fsdp", axis=0, tiled=True),
            lax.all_gather(shards[3], "fsdp", axis=0, tiled=True),
            lax.all_gather(shards[4], "fsdp", axis=0, tiled=True),
            lax.all_gather(shards[5], "fsdp", axis=0, tiled=True),
            lax.all_gather(shards[6], "fsdp", axis=0, tiled=True),
            lax.all_gather(shards[7], "fsdp", axis=0, tiled=True),
            lax.all_gather(shards[8], "fsdp", axis=0, tiled=True),
            lax.all_gather(shards[9], "fsdp", axis=0, tiled=True),
            lax.all_gather(shards[10], "fsdp", axis=0, tiled=True),
            lax.all_gather(shards[11], "fsdp", axis=0, tiled=True),
            lax.all_gather(shards[12], "fsdp", axis=0, tiled=True),
        )
        frame_rows = frames[slot]
        gain_one = whole[0].astype(jnp.float32)
        shift_one = whole[1].astype(jnp.float32)
        norm_a = layer_norm(frame_rows, gain_one, shift_one).astype(jnp.bfloat16)
        qkv = product(norm_a, whole[2])
        query = (qkv[:, :width] + whole[3].astype(jnp.float32)).astype(jnp.bfloat16)
        key = qkv[:, width : 2 * width].astype(jnp.bfloat16)
        value = (qkv[:, 2 * width :] + whole[4].astype(jnp.float32)).astype(jnp.bfloat16)
        keys_all, values_all = (
            lax.all_gather(key, "fsdp", axis=0, tiled=True),
            lax.all_gather(value, "fsdp", axis=0, tiled=True),
        )
        mixed, totals = attend(query, keys_all, values_all, valid)
        attn_in = mixed.astype(jnp.bfloat16)
        resid = frame_rows + product(attn_in, whole[5]) + whole[6].astype(jnp.float32)
        gain_two = whole[7].astype(jnp.float32)
        shift_two = whole[8].astype(jnp.float32)
        norm_f = layer_norm(resid, gain_two, shift_two).astype(jnp.bfloat16)
        upward = product(norm_f, whole[9]) + whole[10].astype(jnp.float32)
        hidden = exact_gelu(upward).astype(jnp.bfloat16)
        outputs.append(resid + product(hidden, whole[11]) + whole[12].astype(jnp.float32))
        whole = (
            lax.all_gather(shards[0], "fsdp", axis=0, tiled=True),
            lax.all_gather(shards[1], "fsdp", axis=0, tiled=True),
            lax.all_gather(shards[2], "fsdp", axis=0, tiled=True),
            lax.all_gather(shards[3], "fsdp", axis=0, tiled=True),
            lax.all_gather(shards[4], "fsdp", axis=0, tiled=True),
            lax.all_gather(shards[5], "fsdp", axis=0, tiled=True),
            lax.all_gather(shards[6], "fsdp", axis=0, tiled=True),
            lax.all_gather(shards[7], "fsdp", axis=0, tiled=True),
            lax.all_gather(shards[8], "fsdp", axis=0, tiled=True),
            lax.all_gather(shards[9], "fsdp", axis=0, tiled=True),
            lax.all_gather(shards[10], "fsdp", axis=0, tiled=True),
            lax.all_gather(shards[11], "fsdp", axis=0, tiled=True),
            lax.all_gather(shards[12], "fsdp", axis=0, tiled=True),
        )
        d_out = cotangent[slot].astype(jnp.bfloat16)
        d_hidden = product_right(d_out, whole[11])
        unused, gelu_back = jax.vjp(exact_gelu, upward)
        d_up = gelu_back(d_hidden)[0].astype(jnp.bfloat16)
        unused, norm_two_back = jax.vjp(layer_norm, resid, gain_two, shift_two)
        d_resid_norm, grad_gain_two, grad_shift_two = norm_two_back(product_right(d_up, whole[9]))
        d_resid = cotangent[slot] + d_resid_norm
        d_attn = d_resid.astype(jnp.bfloat16)
        d_mixed = product_right(d_attn, whole[5]).astype(jnp.bfloat16)
        d_query, key_terms, value_terms = attend_back(
            query, keys_all, values_all, valid, totals, d_mixed
        )
        d_key, d_value = (
            lax.psum_scatter(key_terms, "fsdp", scatter_dimension=0, tiled=True),
            lax.psum_scatter(value_terms, "fsdp", scatter_dimension=0, tiled=True),
        )
        d_query = d_query.astype(jnp.bfloat16)
        d_key = d_key.astype(jnp.bfloat16)
        d_value = d_value.astype(jnp.bfloat16)
        d_qkv = jnp.concatenate([d_query, d_key, d_value], axis=1)
        unused, norm_one_back = jax.vjp(layer_norm, frame_rows, gain_one, shift_one)
        d_frames_norm, grad_gain_one, grad_shift_one = norm_one_back(product_right(d_qkv, whole[2]))
        input_grads.append(d_resid + d_frames_norm)
        pieces = (norm_a, d_qkv, attn_in, d_attn, norm_f, d_up, hidden, d_out)
        smalls = (grad_gain_one, grad_shift_one, grad_gain_two, grad_shift_two)
        kept_pieces.append(pieces)
        small_sum = add_tuples(small_sum, smalls)
    joined = tuple(
        (jnp.concatenate([group[index] for group in kept_pieces], axis=0) for index in range(8))
    )
    owned = lax.psum_scatter(
        weight_grads(joined, small_sum), "fsdp", scatter_dimension=0, tiled=True
    )
    summed = lax.psum(
        (
            owned[0],
            owned[1],
            owned[2],
            owned[3],
            owned[4],
            owned[5],
            owned[6],
            owned[7],
            owned[8],
            owned[9],
            owned[10],
            owned[11],
            owned[12],
        ),
        "rep",
    )
    return (jnp.stack(outputs), jnp.stack(input_grads)) + tuple(summed)


LOW = jnp.bfloat16
FULL = jnp.float32
VMEM = 60 * 2**20


def contract(left, right, left_dim, right_dim):
    return lax.dot_general(
        left, right, (((left_dim,), (right_dim,)), ((), ())), preferred_element_type=FULL
    )


def const_spec(shape):
    return pl.BlockSpec(shape, lambda *at: (0,) * len(shape), pipeline_mode=pl.Buffered(1))


def call(kernel, grid, in_specs, out_specs, out_shape, scratch=(), flops=0, moved=0, exps=0, aliases=None):
    return pl.pallas_call(
        kernel,
        grid_spec=pltpu.PrefetchScalarGridSpec(
            num_scalar_prefetch=1,
            grid=grid,
            in_specs=in_specs,
            out_specs=out_specs,
            scratch_shapes=list(scratch),
        ),
        out_shape=out_shape,
        input_output_aliases=aliases or {},
        compiler_params=pltpu.CompilerParams(vmem_limit_bytes=VMEM),
        cost_estimate=pl.CostEstimate(flops=flops, bytes_accessed=moved, transcendentals=exps),
    )


def spread(rows):
    mean = jnp.mean(rows, axis=-1, keepdims=True)
    centred = rows - mean
    scale = lax.rsqrt(jnp.mean(centred * centred, axis=-1, keepdims=True) + 1e-05)
    return centred * scale, scale


def norm_pull(unit, scale, gain, grad):
    inner = grad * gain
    along = jnp.mean(inner * unit, axis=-1, keepdims=True)
    return scale * (inner - jnp.mean(inner, axis=-1, keepdims=True) - unit * along)


def vector(params_ref, at, half):
    return jnp.concatenate(
        [params_ref[0:1, at : at + half], params_ref[1:2, at : at + half]], axis=1
    )


def struct(shape, dtype):
    return jax.ShapeDtypeStruct(shape, dtype)


def first_norm_kernel(ids, frames_ref, params_ref, norm_ref, low_ref):
    rows = frames_ref[0]
    half = rows.shape[1] // 2
    unit, unused = spread(rows)
    norm_ref[...] = (unit * vector(params_ref, 0, half) + vector(params_ref, half, half)).astype(LOW)
    low_ref[...] = rows.astype(LOW)


def first_norm(ids, frames, params, other):
    unused, rows, width = frames.shape
    block = rows // 2
    return call(
        first_norm_kernel,
        (2,),
        [
            pl.BlockSpec((1, block, width), lambda i, ids: (ids[0] ^ other, i, 0)),
            const_spec(params.shape),
        ],
        [pl.BlockSpec((block, width), lambda i, ids: (i, 0))] * 2,
        [struct((rows, width), LOW)] * 2,
        moved=rows * width * 8,
    )(ids, frames, params)


def place_weights(ids, target, own_ref, piece_refs):
    half = own_ref.shape[0]
    quarter = piece_refs[0].shape[0]
    side, mine = ids[0], ids[1] // 4
    target[pl.ds(pl.multiple_of(side * half, half), half), :] = own_ref[...]
    base = (1 - side) * half
    for turn in range(4):
        at = pl.multiple_of(base + (mine ^ turn) * quarter, quarter)
        target[pl.ds(at, quarter), :] = piece_refs[turn][...]


def project_kernel(ids, own_rows, got_rows, own_ref, p0, p1, p2, p3, bias_ref, out_ref, whole_ref, rows_scr):
    half = own_rows.shape[0]

    @pl.when(pl.program_id(0) == 0)
    def _():
        rows_scr[0:half] = own_rows[...]
        rows_scr[half:] = got_rows[...]

    place_weights(ids, whole_ref, own_ref, (p0, p1, p2, p3))
    out = contract(rows_scr[...], whole_ref[...], 1, 0) + bias_ref[...]
    out_ref[...] = out.astype(LOW)


def project(ids, own_rows, got_rows, own, pieces, bias):
    half, width = own_rows.shape
    columns = own.shape[1]
    tile = 768
    return call(
        project_kernel,
        (columns // tile,),
        [const_spec((half, width))] * 2
        + [pl.BlockSpec((width // 2, tile), lambda j, ids: (0, j))]
        + [pl.BlockSpec((width // 8, tile), lambda j, ids: (0, j))] * 4
        + [pl.BlockSpec((1, tile), lambda j, ids: (0, j))],
        [
            pl.BlockSpec((2 * half, tile), lambda j, ids: (0, j)),
            pl.BlockSpec((width, tile), lambda j, ids: (0, j)),
        ],
        [struct((2 * half, columns), LOW), struct((width, columns), LOW)],
        [pltpu.VMEM((2 * half, width), LOW)],
        flops=4 * half * width * columns,
        moved=2 * (2 * half * width + 2 * half * columns + 2 * width * columns),
    )(ids, own_rows, got_rows, own, *pieces, bias)


def window(head, size):
    first = head * size // 128
    last = -(-(head + 1) * size // 128)
    return first * 128, last * 128, head * size - first * 128


def head_lanes(lanes, offset, size):
    lane = lax.broadcasted_iota(jnp.int32, (1, lanes), 1)
    return (lane >= offset) & (lane < offset + size)


def attend_kernel(size, per, ids, query_ref, key_ref, value_ref, bias_ref, out_ref, total_ref, acc):
    scale = size ** (-0.5)
    bias = bias_ref[...]
    lane = lax.broadcasted_iota(jnp.int32, (1, 128), 1)
    acc[...] = jnp.zeros_like(acc)
    stats = jnp.zeros((query_ref.shape[0], 128), FULL)
    for head in range(per):
        low, high, offset = window(head, size)
        inside = head_lanes(high - low, offset, size)
        query = query_ref[:, low:high]
        query = jnp.where(inside, query, jnp.zeros_like(query))
        scores = contract(query, key_ref[:, low:high], 1, 1) * scale + bias
        peak = jnp.max(scores, axis=-1, keepdims=True)
        raised = jnp.exp(scores - peak)
        summed = jnp.sum(raised, axis=-1, keepdims=True)
        probs = (raised * (1.0 / summed)).astype(LOW)
        mixed = contract(probs, value_ref[:, low:high], 1, 0)
        acc[:, low:high] += jnp.where(inside, mixed, 0.0)
        stats = jnp.where(lane == head, peak + jnp.log(summed), stats)
    out_ref[...] = acc[...].astype(LOW)
    total_ref[...] = stats.T[:per]


def attend_rows(ids, qkv, bias, tile=512, groups=2):
    rows, width = qkv.shape[0], qkv.shape[1] // 3
    size, per, part = width // HEADS, HEADS // groups, width // groups
    return call(
        functools.partial(attend_kernel, size, per),
        (groups, rows // tile),
        [
            pl.BlockSpec((tile, part), lambda g, i, ids: (i, g)),
            pl.BlockSpec((rows, part), lambda g, i, ids: (0, groups + g)),
            pl.BlockSpec((rows, part), lambda g, i, ids: (0, 2 * groups + g)),
            const_spec((1, rows)),
        ],
        [
            pl.BlockSpec((tile, part), lambda g, i, ids: (i, g)),
            pl.BlockSpec((per, tile), lambda g, i, ids: (g, i)),
        ],
        [struct((rows, width), LOW), struct((HEADS, rows), FULL)],
        [pltpu.VMEM((tile, part), FULL)],
        flops=12 * rows * rows * width,
        moved=8 * rows * width,
        exps=HEADS * rows * rows,
    )(ids, qkv, qkv, qkv, bias)


def attend_back_kernel(
    size, per, ids, query_ref, key_ref, value_ref, upper_ref, bias_ref, total_ref, grad_ref, acc, key_sum, value_sum
):
    step = pl.program_id(1)
    scale = size ** (-0.5)
    bias = bias_ref[...]
    tile = query_ref.shape[0]

    @pl.when(step == 0)
    def _():
        key_sum[...] = jnp.zeros_like(key_sum)
        value_sum[...] = jnp.zeros_like(value_sum)

    acc[...] = jnp.zeros_like(acc)
    for head in range(per):
        low, high, offset = window(head, size)
        inside = head_lanes(high - low, offset, size)
        query = query_ref[:, low:high]
        query = jnp.where(inside, query, jnp.zeros_like(query))
        upper = upper_ref[:, low:high]
        upper = jnp.where(inside, upper, jnp.zeros_like(upper))
        keys = key_ref[:, low:high]
        scores = contract(keys, query, 1, 1) * scale + bias
        probs = jnp.exp(scores - total_ref[head : head + 1, :])
        d_probs = contract(value_ref[:, low:high], upper, 1, 1)
        terms = probs * d_probs
        d_scores = (terms - probs * jnp.sum(terms, axis=0, keepdims=True)).astype(LOW)
        value_sum[:, low:high] += contract(probs.astype(LOW), upper, 1, 0)
        key_sum[:, low:high] += contract(d_scores, query, 1, 0)
        acc[:, low:high] += jnp.where(inside, contract(d_scores, keys, 0, 0), 0.0)
    grad_ref[0, pl.ds(pl.multiple_of(step * tile, tile), tile), :] = (acc[...] * scale).astype(LOW)

    @pl.when(step == pl.num_programs(1) - 1)
    def _():
        grad_ref[1] = (key_sum[...] * scale).astype(LOW)
        grad_ref[2] = value_sum[...].astype(LOW)


def attend_back_rows(ids, qkv, upper, bias, totals, tile=512, groups=2):
    rows, width = upper.shape
    size, per, part = width // HEADS, HEADS // groups, width // groups
    return call(
        functools.partial(attend_back_kernel, size, per),
        (groups, rows // tile),
        [
            pl.BlockSpec((tile, part), lambda g, i, ids: (i, g)),
            pl.BlockSpec((rows, part), lambda g, i, ids: (0, groups + g)),
            pl.BlockSpec((rows, part), lambda g, i, ids: (0, 2 * groups + g)),
            pl.BlockSpec((tile, part), lambda g, i, ids: (i, g)),
            const_spec((rows, 1)),
            pl.BlockSpec((per, tile), lambda g, i, ids: (g, i)),
        ],
        pl.BlockSpec((3, rows, part), lambda g, i, ids: (0, 0, g)),
        struct((3, rows, width), LOW),
        [pltpu.VMEM((tile, part), FULL), pltpu.VMEM((rows, part), FULL), pltpu.VMEM((rows, part), FULL)],
        flops=24 * rows * rows * width,
        moved=14 * rows * width,
        exps=HEADS * rows * rows,
    )(ids, qkv, qkv, qkv, upper, bias, totals)


def out_kernel(ids, mixed_ref, own_ref, p0, p1, p2, p3, frames_ref, got_ref, params_ref, resid_ref, norm_ref, whole_ref):
    step = pl.program_id(0)
    half = own_ref.shape[0]

    @pl.when(step == 0)
    def _():
        place_weights(ids, whole_ref, own_ref, (p0, p1, p2, p3))

    near = (step < pl.num_programs(0) // 2).astype(FULL)
    start = frames_ref[0] * near + got_ref[...].astype(FULL) * (1.0 - near)
    resid = start + contract(mixed_ref[...], whole_ref[...], 1, 0) + vector(params_ref, 4 * half, half)
    resid_ref[...] = resid
    unit, unused = spread(resid)
    norm_ref[...] = (unit * vector(params_ref, 5 * half, half) + vector(params_ref, 6 * half, half)).astype(LOW)


def near_spec(tile, width, count):
    return pl.BlockSpec((1, tile, width), lambda i, ids: (ids[0], jnp.minimum(i, count // 2 - 1), 0))


def far_spec(tile, width, count):
    return pl.BlockSpec((tile, width), lambda i, ids: (jnp.maximum(i - count // 2, 0), 0))


def row_spec(tile, width):
    return pl.BlockSpec((tile, width), lambda i, ids: (i, 0))


def out_rows(ids, mixed, own, pieces, frames, got, params, tile=256):
    rows, width = mixed.shape
    count = rows // tile
    piece = pl.BlockSpec((width // 8, width), lambda i, ids: (0, 4), pipeline_mode=pl.Buffered(1))
    return call(
        out_kernel,
        (count,),
        [row_spec(tile, width), const_spec((width // 2, width))]
        + [piece] * 4
        + [near_spec(tile, width, count), far_spec(tile, width, count), const_spec(params.shape)],
        [row_spec(tile, width), row_spec(tile, width), const_spec((width, width))],
        [struct((rows, width), FULL), struct((rows, width), LOW), struct((width, width), LOW)],
        flops=2 * rows * width * width,
        moved=rows * width * 12 + width * width * 4,
    )(ids, mixed, own, *pieces, frames, got, params)


def bell_parts(values):
    bell = jnp.exp(values * values * -0.5)
    return 0.5 + 0.5 * lax.erf(values * (0.5**0.5)), bell


def put_pieces(ids, keep_ref, send_ref, source, block):
    count = keep_ref.shape[1]
    for far in range(2):
        for turn in range(2 * count):
            piece = (ids[0] ^ far) * 2 * count + (ids[1] ^ turn)
            rows = source[pl.ds(pl.multiple_of(piece * block, block), block), :].astype(LOW)
            if turn < count:
                keep_ref[far, turn] = rows
            else:
                send_ref[far, turn - count] = rows


def feed_kernel(
    far, tiles, ids, norm_ref, cot_ref, got_ref, resid_ref, own_ref, p0, p1, p2, p3, *refs
):
    if far:
        d0, d1, d2, d3, params_ref = refs[:5]
        refs = refs[5:]
    else:
        down_ref, params_ref = refs[:2]
        refs = refs[2:]
    y_ref, dn_ref, keep_ref, send_ref, down_keep, down_send, bias_ref, up_w, down_w, norm_t, grad, grad_low, dout = refs
    step = pl.program_id(0)
    half = own_ref.shape[0]
    tile = own_ref.shape[1]
    rows = norm_ref.shape[0]

    @pl.when(step == 0)
    def _():
        if far:
            y_ref[...] = jnp.zeros_like(y_ref)
        else:
            y_ref[...] = resid_ref[...] + vector(params_ref, 7 * half, half)
        dn_ref[...] = jnp.zeros_like(dn_ref)
        norm_t[...] = norm_ref[...].T
        dout[: rows // 2] = cot_ref[0].astype(LOW)
        dout[rows // 2 :] = got_ref[...]

    place_weights(ids, up_w, own_ref, (p0, p1, p2, p3))
    if far:
        part = tile // 4
        mine = ids[1] // 4
        for turn, ref in enumerate((d0, d1, d2, d3)):
            down_w[pl.ds(pl.multiple_of((mine ^ turn) * part, part), part), :] = ref[0]
        down = down_w[...]
    else:
        down = down_ref[...]
    up = up_w[...]
    upper = dout[...]
    at = pl.multiple_of(8 * half + step * tile, tile)
    side = (ids[0] ^ far) == 0
    bias = jnp.where(side, params_ref[0:1, pl.ds(at, tile)], params_ref[1:2, pl.ds(at, tile)])
    raised = contract(norm_ref[...], up, 1, 0) + bias
    d_hidden = contract(upper, down, 1, 1)
    lower, bell = bell_parts(raised)
    hidden = (raised * lower).astype(LOW)
    d_up = (d_hidden * (lower + raised * bell * (0.5 / jnp.pi) ** 0.5)).astype(LOW)
    bias_ref[...] = jnp.sum(d_up.astype(FULL), axis=0, keepdims=True)
    y_ref[...] += contract(hidden, down, 1, 0)
    dn_ref[...] += contract(d_up, up, 1, 1)
    grad[...] = contract(norm_t[...], d_up, 1, 0)
    put_pieces(ids, keep_ref, send_ref, grad, keep_ref.shape[2])
    grad_low[...] = contract(hidden, upper, 0, 0)
    count, block = down_keep.shape[0], down_keep.shape[1]
    for turn in range(2 * count):
        low = grad_low[pl.ds(pl.multiple_of((ids[1] ^ turn) * block, block), block), :].astype(LOW)
        if turn < count:
            down_keep[turn] = low
        else:
            down_send[turn - count] = low


def feed_rows(far, ids, norm, cotangent, got, resid, own, pieces, down, params, tile=512):
    rows, width = norm.shape
    half = own.shape[1] // 2
    tiles = half // tile
    side = lambda ids: ids[0] ^ far
    own_spec = pl.BlockSpec((width // 2, tile), lambda j, ids: (0, side(ids) * tiles + j))
    piece_spec = pl.BlockSpec((width // 8, tile), lambda j, ids: (0, side(ids) * tiles + j))
    if far:
        down_specs = [pl.BlockSpec((1, tile // 4, width), lambda j, ids: (j, 0, 0))] * 4
    else:
        down_specs = [pl.BlockSpec((tile, width), lambda j, ids: (j, 0))]
        down = (down,)
    block, fine = width // 32, tile // 16
    return call(
        functools.partial(feed_kernel, far, tiles),
        (tiles,),
        [
            const_spec((rows, width)),
            pl.BlockSpec((1, rows // 2, width), lambda j, ids: (ids[0], 0, 0), pipeline_mode=pl.Buffered(1)),
            const_spec((rows // 2, width)),
            const_spec((rows, width)) if not far else const_spec((8, width)),
            own_spec,
        ]
        + [piece_spec] * 4
        + down_specs
        + [const_spec(params.shape)],
        [
            const_spec((rows, width)),
            const_spec((rows, width)),
            pl.BlockSpec((2, 8, block, tile), lambda j, ids: (0, 0, 0, j)),
            pl.BlockSpec((2, 8, block, tile), lambda j, ids: (0, 0, 0, j)),
            pl.BlockSpec((8, fine, width), lambda j, ids: (0, j, 0)),
            pl.BlockSpec((8, fine, width), lambda j, ids: (0, j, 0)),
            pl.BlockSpec((1, tile), lambda j, ids: (0, j)),
        ],
        [struct((rows, width), FULL)] * 2
        + [struct((2, 8, block, half), LOW)] * 2
        + [struct((8, half // 16, width), LOW)] * 2
        + [struct((1, half), FULL)],
        [
            pltpu.VMEM((width, tile), LOW),
            pltpu.VMEM((tile, width), LOW),
            pltpu.VMEM((width, rows), LOW),
            pltpu.VMEM((width, tile), FULL),
            pltpu.VMEM((tile, width), FULL),
            pltpu.VMEM((rows, width), LOW),
        ],
        flops=12 * rows * width * half,
        moved=rows * width * 14 + width * half * 8,
        exps=2 * rows * half,
    )(ids, norm, cotangent, got, resid, own, *pieces, *down, params)


def middle_kernel(
    ids, y0_ref, y1_ref, dn0_ref, dn1_ref, resid_ref, cot_ref, got_ref, mixed_ref, whole_ref, params_ref,
    near_ref, far_ref, d_resid_ref, d_mixed_ref, keep_ref, send_ref, small_ref, grad, sums,
):
    step = pl.program_id(0)
    count = pl.num_programs(0)
    half = params_ref.shape[1] // 12

    @pl.when(step == 0)
    def _():
        grad[...] = jnp.zeros_like(grad)
        sums[...] = jnp.zeros_like(sums)

    out = y0_ref[...] + y1_ref[...]
    is_near = step < count // 2

    @pl.when(is_near)
    def _():
        near_ref[0] = out

    @pl.when(jnp.logical_not(is_near))
    def _():
        far_ref[...] = out.astype(LOW)

    pick = is_near.astype(FULL)
    cot = cot_ref[0] * pick + got_ref[...].astype(FULL) * (1.0 - pick)
    d_norm = dn0_ref[...] + dn1_ref[...]
    unit, scale = spread(resid_ref[...])
    d_resid = cot + norm_pull(unit, scale, vector(params_ref, 5 * half, half), d_norm)
    d_attn = d_resid.astype(LOW)
    d_resid_ref[...] = d_resid
    d_mixed_ref[...] = contract(d_attn, whole_ref[...], 1, 1).astype(LOW)
    grad[...] += contract(mixed_ref[...], d_attn, 0, 0)
    sums[0:1] += jnp.sum(d_attn.astype(FULL), axis=0, keepdims=True)
    sums[1:2] += jnp.sum(d_norm * unit, axis=0, keepdims=True)
    sums[2:3] += jnp.sum(d_norm, axis=0, keepdims=True)
    sums[3:4] += jnp.sum(cot.astype(LOW).astype(FULL), axis=0, keepdims=True)

    @pl.when(step == count - 1)
    def _():
        put_pieces(ids, keep_ref, send_ref, grad, keep_ref.shape[2])
        small_ref[...] = sums[...]


def middle_rows(ids, y0, y1, dn0, dn1, resid, cotangent, got, mixed, whole, params, tile=256):
    rows, width = mixed.shape
    count = rows // tile
    wide = row_spec(tile, width)
    piece = const_spec((2, 8, width // 32, width))
    return call(
        middle_kernel,
        (count,),
        [wide] * 5
        + [near_spec(tile, width, count), far_spec(tile, width, count), wide, const_spec((width, width)), const_spec(params.shape)],
        [near_spec(tile, width, count), far_spec(tile, width, count), wide, wide, piece, piece, const_spec((8, width))],
        [
            struct(cotangent.shape, FULL),
            struct((rows // 2, width), LOW),
            struct((rows, width), FULL),
            struct((rows, width), LOW),
            struct((2, 8, width // 32, width), LOW),
            struct((2, 8, width // 32, width), LOW),
            struct((8, width), FULL),
        ],
        [pltpu.VMEM((width, width), FULL), pltpu.VMEM((8, width), FULL)],
        flops=4 * rows * width * width,
        moved=rows * width * 36 + width * width * 4,
    )(ids, y0, y1, dn0, dn1, resid, cotangent, got, mixed, whole, params)


def project_grad_kernel(ids, own_rows, got_rows, grad_ref, keep_ref, send_ref, bias_ref, norm_t, grad):
    half = own_rows.shape[0]

    @pl.when(pl.program_id(0) == 0)
    def _():
        norm_t[:, :half] = own_rows[...].T
        norm_t[:, half:] = got_rows[...].T

    d_part = grad_ref[0]
    grad[...] = contract(norm_t[...], d_part, 1, 0)
    put_pieces(ids, keep_ref, send_ref, grad, keep_ref.shape[2])
    bias_ref[0] = jnp.sum(d_part.astype(FULL), axis=0, keepdims=True)


def project_grad(ids, own_rows, got_rows, d_qkv):
    half, width = own_rows.shape
    piece = pl.BlockSpec((2, 8, width // 32, width), lambda j, ids: (0, 0, 0, j))
    return call(
        project_grad_kernel,
        (3,),
        [const_spec((half, width))] * 2 + [pl.BlockSpec((1, 2 * half, width), lambda j, ids: (j, 0, 0))],
        [piece, piece, pl.BlockSpec((1, 1, width), lambda j, ids: (j, 0, 0))],
        [struct((2, 8, width // 32, 3 * width), LOW)] * 2 + [struct((3, 1, width), FULL)],
        [pltpu.VMEM((width, 2 * half), LOW), pltpu.VMEM((width, width), FULL)],
        flops=12 * half * width * width,
        moved=16 * half * width + 6 * width * width,
    )(ids, own_rows, got_rows, d_qkv)


def last_kernel(ids, d_qkv_ref, whole_ref, frames_ref, low_ref, d_resid_ref, params_ref, near_ref, far_ref, small_ref, sums):
    step = pl.program_id(0)
    count = pl.num_programs(0)
    half = params_ref.shape[1] // 12
    width = 2 * half

    @pl.when(step == 0)
    def _():
        sums[...] = jnp.zeros_like(sums)

    d_norm = contract(d_qkv_ref[0], whole_ref[:, :width], 1, 1)
    d_norm += contract(d_qkv_ref[1], whole_ref[:, width : 2 * width], 1, 1)
    d_norm += contract(d_qkv_ref[2], whole_ref[:, 2 * width :], 1, 1)
    is_near = step < count // 2
    pick = is_near.astype(FULL)
    rows = frames_ref[0] * pick + low_ref[...].astype(FULL) * (1.0 - pick)
    unit, scale = spread(rows)
    grad = d_resid_ref[...] + norm_pull(unit, scale, vector(params_ref, 0, half), d_norm)
    sums[0:1] += jnp.sum(d_norm * unit, axis=0, keepdims=True)
    sums[1:2] += jnp.sum(d_norm, axis=0, keepdims=True)

    @pl.when(is_near)
    def _():
        near_ref[0] = grad

    @pl.when(jnp.logical_not(is_near))
    def _():
        far_ref[...] = grad.astype(LOW)

    @pl.when(step == count - 1)
    def _():
        small_ref[...] = sums[...]


def last_rows(ids, d_qkv, whole, frames, low, d_resid, params, tile=256):
    rows, width = d_resid.shape
    count = rows // tile
    return call(
        last_kernel,
        (count,),
        [
            pl.BlockSpec((3, tile, width), lambda i, ids: (0, i, 0)),
            const_spec((width, 3 * width)),
            near_spec(tile, width, count),
            far_spec(tile, width, count),
            row_spec(tile, width),
            const_spec(params.shape),
        ],
        [near_spec(tile, width, count), far_spec(tile, width, count), const_spec((8, width))],
        [struct(frames.shape, FULL), struct((rows // 2, width), LOW), struct((8, width), FULL)],
        [pltpu.VMEM((8, width), FULL)],
        flops=6 * rows * width * width,
        moved=rows * width * 18 + width * width * 6,
    )(ids, d_qkv, whole, frames, low, d_resid, params)


def fill_kernel(ids, whole_ref, part_ref, out_ref):
    out_ref[0] = part_ref[...].astype(FULL)


def fill_rows(ids, whole, part):
    rows, width = part.shape
    tile = rows // 2
    return call(
        fill_kernel,
        (2,),
        [pl.BlockSpec(memory_space=pl.ANY), pl.BlockSpec((tile, width), lambda i, ids: (i, 0))],
        pl.BlockSpec((1, tile, width), lambda i, ids: (1 - ids[0], i, 0)),
        struct(whole.shape, FULL),
        moved=rows * width * 6,
        aliases={1: 0},
    )(ids, whole, part)


def settle_kernel(ids, *refs):
    out_ref = refs[-1]
    step = pl.program_id(0)
    for at in range(len(refs) // 2):
        keep_ref, got_ref = refs[2 * at], refs[2 * at + 1]

        @pl.when((step >= 16 * at) & (step < 16 * at + 8))
        def _():
            out_ref[...] = keep_ref[...].reshape(out_ref.shape).astype(FULL)

        @pl.when((step >= 16 * at + 8) & (step < 16 * at + 16))
        def _():
            out_ref[...] = got_ref[...].reshape(out_ref.shape).astype(FULL)


def settle(ids, pairs, shape, block, place):
    count, rows, columns = pairs[0][0].shape
    specs = []
    for at in range(len(pairs)):
        for side in range(2):
            first = 16 * at + 8 * side
            specs.append(
                pl.BlockSpec((1, rows, columns), lambda s, ids, first=first: (jnp.clip(s - first, 0, 7), 0, 0))
            )
    return call(
        settle_kernel,
        (16 * len(pairs),),
        specs,
        pl.BlockSpec(block, lambda s, ids: place(ids, s // 16, (s % 16) ^ ids[1])),
        struct(shape, FULL),
        moved=len(pairs) * 16 * rows * columns * 6,
    )(ids, *[array for pair in pairs for array in pair])


CORE, Y, NEAR_Z, FAR_Z = 1, 2, 4, 8


def swap(array, bit):
    return lax.ppermute(array, "rep", [(at, at ^ bit) for at in range(16)])


def cross(array):
    return lax.ppermute(array, "fsdp", [(0, 1), (1, 0)])


def plus(first, second):
    return first.astype(FULL) + second.astype(FULL)


def reduce_pieces(keep_near, keep_far, send_near, send_far):
    got_far = swap(send_far, CORE)
    got_near = swap(send_near, CORE)
    over = cross(plus(keep_far, got_far).astype(LOW))
    total = plus(keep_near, got_near) + over.astype(FULL)
    return reduce_rest(total)


def reduce_rest(total):
    for bit in (Y, NEAR_Z, FAR_Z):
        half = total.shape[0] // 2
        got = swap(total[half:].astype(LOW), bit)
        total = plus(total[:half], got)
    return total.astype(LOW)


def gather_pieces(piece):
    for bit in (FAR_Z, NEAR_Z, Y):
        piece = jnp.concatenate([piece, swap(piece, bit)], axis=0)
    return piece, swap(piece, CORE)


def fetch(piece):
    first = cross(piece)
    second = swap(first, Y)
    return first, second, swap(first, CORE), swap(second, CORE)


def paired_device(
    frames, cotangent, clip_lengths, clip_slots, gain_attn, shift_attn, w_qkv, bias_query, bias_value,
    w_out, bias_out, gain_ffn, shift_ffn, w_up, bias_up, w_down, bias_down,
):
    unused, rows, width = frames.shape
    half = width // 2
    quarter = half // 4
    side = lax.axis_index("fsdp")
    at = lax.axis_index("rep")
    mine = ((at & 1) << 3) | ((at & 2) << 1) | ((at & 4) >> 1) | ((at & 8) >> 3)
    ids = jnp.stack([side, mine]).astype(jnp.int32)
    fourth = mine // 4

    own_small = jnp.concatenate(
        [gain_attn, shift_attn, bias_query, bias_value, bias_out, gain_ffn, shift_ffn, bias_down, bias_up]
    )[None]
    got_small = cross(own_small)
    params = jnp.concatenate(
        [jnp.where(side == 0, own_small, got_small), jnp.where(side == 0, got_small, own_small)], axis=0
    ).astype(FULL)

    def piece_of(weight):
        return lax.dynamic_slice_in_dim(weight, fourth * quarter, quarter, axis=0)

    pieces_qkv = fetch(piece_of(w_qkv))
    send_norm, send_low = first_norm(ids, frames, params, 1)
    own_norm, unused = first_norm(ids, frames, params, 0)
    got_norm = cross(send_norm)
    got_low = cross(send_low)
    got_cot = cross(lax.dynamic_index_in_dim(cotangent, 1 - side, 0, keepdims=False).astype(LOW))
    pieces_up = fetch(jnp.concatenate([piece_of(w_up), piece_of(w_out)], axis=1))
    tile = 512
    tiles = w_down.shape[0] // tile
    pieces_down = fetch(
        lax.dynamic_index_in_dim(w_down.reshape(tiles, 4, tile // 4, width), fourth, 1, keepdims=False)
    )

    bias_qkv = jnp.concatenate(
        [params[:, 2 * half : 3 * half].reshape(1, width), jnp.zeros((1, width), FULL), params[:, 3 * half : 4 * half].reshape(1, width)],
        axis=1,
    )
    slot = lax.dynamic_index_in_dim(clip_slots, side, 0, keepdims=False)
    numbers = jnp.arange(clip_lengths.shape[0], dtype=jnp.int32)
    span = jnp.sum(jnp.where(numbers == slot, clip_lengths, 0))
    place = jnp.arange(2 * rows, dtype=jnp.int32)
    place = jnp.where(place < rows, place + side * rows, place - rows + (1 - side) * rows)
    mask = jnp.where(place < span, 0.0, -1e30).astype(FULL)

    qkv, whole_qkv = project(ids, own_norm, got_norm, w_qkv, pieces_qkv, bias_qkv)
    mixed, totals = attend_rows(ids, qkv, mask[None])
    resid, norm_f, whole_out = out_rows(ids, mixed, w_out, pieces_up, frames, got_low, params)
    y0, dn0, up_keep0, up_send0, down_keep0, down_send0, bias0 = feed_rows(
        0, ids, norm_f, cotangent, got_cot, resid, w_up, pieces_up, w_down, params
    )
    y1, dn1, up_keep1, up_send1, down_keep1, down_send1, bias1 = feed_rows(
        1, ids, norm_f, cotangent, got_cot, resid, w_up, pieces_up, pieces_down, params
    )
    up0 = gather_pieces(reduce_pieces(up_keep0[0], up_keep1[1], up_send0[0], up_send1[1]))
    up1 = gather_pieces(reduce_pieces(up_keep1[0], up_keep0[1], up_send1[0], up_send0[1]))
    down = gather_pieces(reduce_pieces(down_keep0, down_keep1, down_send0, down_send1))
    output, far_out, d_resid, d_mixed, out_keep, out_send, small_mid = middle_rows(
        ids, y0, y1, dn0, dn1, resid, cotangent, got_cot, mixed, whole_out, params
    )
    out = gather_pieces(reduce_pieces(out_keep[0], out_keep[1], out_send[0], out_send[1]))
    output = fill_rows(ids, output, cross(far_out))
    d_qkv = attend_back_rows(ids, qkv, d_mixed, mask[:, None], totals)
    qkv_keep, qkv_send, small_qkv = project_grad(ids, own_norm, got_norm, d_qkv)
    qkv_grad = gather_pieces(reduce_pieces(qkv_keep[0], qkv_keep[1], qkv_send[0], qkv_send[1]))
    frames_grad, far_grad, small_last = last_rows(ids, d_qkv, whole_qkv, frames, got_low, d_resid, params)
    frames_grad = fill_rows(ids, frames_grad, cross(far_grad))

    bias_up_sum = jnp.where(side == 0, jnp.concatenate([bias0, bias1]), jnp.concatenate([bias1, bias0]))
    vectors = [small_last[0], small_last[1], small_qkv[0, 0], small_qkv[2, 0], small_mid[0], small_mid[1], small_mid[2], small_mid[3]]
    small = jnp.concatenate([v.reshape(2, half) for v in vectors] + [bias_up_sum], axis=1)
    got = cross(lax.dynamic_slice_in_dim(small, 1 - side, 1, axis=0))
    small = lax.dynamic_slice_in_dim(small, side, 1, axis=0) + got
    for bit in (CORE, Y, NEAR_Z, FAR_Z):
        small = small + swap(small, bit)
    small = small[0]
    parts = [small[k * half : (k + 1) * half] for k in range(8)] + [small[8 * half :]]

    def row_place(ids, part, piece):
        return (piece, 0, 0)

    block = half // 16
    qkv_out = settle(ids, [qkv_grad], (16, block, 3 * width), (1, block, 3 * width), row_place)
    out_out = settle(ids, [out], (16, block, width), (1, block, width), row_place)
    ff = w_up.shape[1]
    up_out = settle(
        ids, [up0, up1], (16, block, ff), (1, block, ff // 2), lambda ids, part, piece: (piece, 0, part ^ ids[0])
    )
    down_out = settle(
        ids, [down], (tiles, 16, tile // 16, width), (tiles, 1, tile // 16, width), lambda ids, part, piece: (0, piece, 0, 0)
    )
    return (
        output,
        frames_grad,
        parts[0],
        parts[1],
        qkv_out.reshape(half, 3 * width),
        parts[2],
        parts[3],
        out_out.reshape(half, width),
        parts[4],
        parts[5],
        parts[6],
        up_out.reshape(half, ff),
        parts[8],
        down_out.reshape(ff // 2, width),
        parts[7],
    )


def solution(mesh):
    fast = mesh.shape["fsdp"] == 2 and mesh.shape["rep"] == 16
    return jax.shard_map(
        paired_device if fast else general_device,
        mesh=mesh,
        in_specs=(
            P("rep", "fsdp", None),
            P("rep", "fsdp", None),
            P(),
            P("rep"),
            P("fsdp"),
            P("fsdp"),
            P("fsdp", None),
            P("fsdp"),
            P("fsdp"),
            P("fsdp", None),
            P("fsdp"),
            P("fsdp"),
            P("fsdp"),
            P("fsdp", None),
            P("fsdp"),
            P("fsdp", None),
            P("fsdp"),
        ),
        out_specs=(
            P("rep", "fsdp", None),
            P("rep", "fsdp", None),
            P("fsdp"),
            P("fsdp"),
            P("fsdp", None),
            P("fsdp"),
            P("fsdp"),
            P("fsdp", None),
            P("fsdp"),
            P("fsdp"),
            P("fsdp"),
            P("fsdp", None),
            P("fsdp"),
            P("fsdp", None),
            P("fsdp"),
        ),
        check_vma=False,
    )
```

```python
import functools

import jax
import jax.numpy as jnp
from jax import lax
from jax.experimental import pallas as pl
from jax.experimental.pallas import tpu as pltpu
from jax.sharding import PartitionSpec as P

HEADS = 16


def layer_norm(rows, gain, shift):
    mean = jnp.mean(rows, axis=-1, keepdims=True)
    centred = rows - mean
    spread = jnp.mean(centred * centred, axis=-1, keepdims=True)
    return centred * lax.rsqrt(spread + 1e-05) * gain + shift


def exact_gelu(values):
    return jax.nn.gelu(values, approximate=False)


def product(left, right):
    return jnp.dot(left, right, preferred_element_type=jnp.float32)


def product_left(left, right):
    return lax.dot_general(
        left, right, (((0,), (0,)), ((), ())), preferred_element_type=jnp.float32
    )


def product_right(left, right):
    return lax.dot_general(
        left, right, (((1,), (1,)), ((), ())), preferred_element_type=jnp.float32
    )


def head_blocks(query, keys, values, block):
    rows, width = query.shape
    half = width // 2
    per = HEADS // 2
    size = width // HEADS
    lower = block * half
    query_part = query[:, lower : lower + half].reshape(rows, per, size)
    key_part = keys[:, lower : lower + half].reshape(keys.shape[0], per, size)
    value_part = values[:, lower : lower + half].reshape(values.shape[0], per, size)
    return (query_part, key_part, value_part)


def masked_scores(query_part, key_part, valid, scale):
    scores = (
        jnp.einsum("qhd,khd->hqk", query_part, key_part, preferred_element_type=jnp.float32) * scale
    )
    return jnp.where(valid[None, None, :], scores, -1e30)


def attend(query, keys, values, valid):
    rows, width = query.shape
    scale = (width // HEADS) ** (-0.5)
    pieces = []
    totals = []
    for block in range(2):
        query_part, key_part, value_part = head_blocks(query, keys, values, block)
        scores = masked_scores(query_part, key_part, valid, scale)
        peak = jnp.max(scores, axis=-1, keepdims=True)
        raised = jnp.exp(scores - peak)
        summed = jnp.sum(raised, axis=-1, keepdims=True)
        probs = (raised / summed).astype(jnp.bfloat16)
        mixed = jnp.einsum("hqk,khd->qhd", probs, value_part, preferred_element_type=jnp.float32)
        pieces.append(mixed.reshape(rows, width // 2))
        totals.append(peak + jnp.log(summed))
    return (jnp.concatenate(pieces, axis=1), totals)


def attend_back(query, keys, values, valid, totals, d_mixed):
    rows, width = query.shape
    scale = (width // HEADS) ** (-0.5)
    query_grads = []
    key_grads = []
    value_grads = []
    for block in range(2):
        query_part, key_part, value_part = head_blocks(query, keys, values, block)
        upper = d_mixed[:, block * (width // 2) : (block + 1) * (width // 2)].reshape(
            query_part.shape
        )
        scores = masked_scores(query_part, key_part, valid, scale)
        probs = jnp.exp(scores - totals[block])
        d_probs = jnp.einsum("qhd,khd->hqk", upper, value_part, preferred_element_type=jnp.float32)
        centre = jnp.sum(probs * d_probs, axis=-1, keepdims=True)
        d_scores = (probs * (d_probs - centre)).astype(jnp.bfloat16)
        d_query = (
            jnp.einsum("hqk,khd->qhd", d_scores, key_part, preferred_element_type=jnp.float32)
            * scale
        )
        d_key = (
            jnp.einsum("hqk,qhd->khd", d_scores, query_part, preferred_element_type=jnp.float32)
            * scale
        )
        d_value = jnp.einsum(
            "hqk,qhd->khd", probs.astype(jnp.bfloat16), upper, preferred_element_type=jnp.float32
        )
        query_grads.append(d_query.reshape(rows, width // 2))
        key_grads.append(d_key.reshape(keys.shape[0], width // 2))
        value_grads.append(d_value.reshape(keys.shape[0], width // 2))
    return (
        jnp.concatenate(query_grads, axis=1),
        jnp.concatenate(key_grads, axis=1),
        jnp.concatenate(value_grads, axis=1),
    )


def add_tuples(first, second):
    if first is None:
        return second
    return tuple((left + right for left, right in zip(first, second)))


def weight_grads(pieces, smalls):
    norm_a, d_qkv, attn_in, d_attn, norm_f, d_up, hidden, d_out = pieces
    gain_one, shift_one, gain_two, shift_two = smalls
    width = norm_a.shape[1]
    grad_qkv = product_left(norm_a, d_qkv)
    columns = jnp.sum(d_qkv.astype(jnp.float32), axis=0)
    grad_query_bias = columns[:width]
    grad_value_bias = columns[2 * width :]
    grad_out = product_left(attn_in, d_attn)
    grad_out_bias = jnp.sum(d_attn.astype(jnp.float32), axis=0)
    grad_up = product_left(norm_f, d_up)
    grad_up_bias = jnp.sum(d_up.astype(jnp.float32), axis=0)
    grad_down = product_left(hidden, d_out)
    grad_down_bias = jnp.sum(d_out.astype(jnp.float32), axis=0)
    return (
        gain_one,
        shift_one,
        grad_qkv,
        grad_query_bias,
        grad_value_bias,
        grad_out,
        grad_out_bias,
        gain_two,
        shift_two,
        grad_up,
        grad_up_bias,
        grad_down,
        grad_down_bias,
    )


def general_device(
    frames,
    cotangent,
    clip_lengths,
    clip_slots,
    gain_attn,
    shift_attn,
    w_qkv,
    bias_query,
    bias_value,
    w_out,
    bias_out,
    gain_ffn,
    shift_ffn,
    w_up,
    bias_up,
    w_down,
    bias_down,
):
    shards = (
        gain_attn,
        shift_attn,
        w_qkv,
        bias_query,
        bias_value,
        w_out,
        bias_out,
        gain_ffn,
        shift_ffn,
        w_up,
        bias_up,
        w_down,
        bias_down,
    )
    micro, rows, width = frames.shape
    group_size = lax.axis_size("fsdp")
    length_all = rows * group_size
    positions = jnp.arange(length_all, dtype=jnp.int32)
    numbers = jnp.arange(clip_lengths.shape[0], dtype=jnp.int32)
    outputs = []
    input_grads = []
    summed = None
    kept_pieces = []
    small_sum = None
    for slot in range(micro):
        span = jnp.sum(jnp.where(numbers == clip_slots[slot], clip_lengths, 0))
        valid = positions < span
        whole = (
            lax.all_gather(shards[0], "fsdp", axis=0, tiled=True),
            lax.all_gather(shards[1], "fsdp", axis=0, tiled=True),
            lax.all_gather(shards[2], "fsdp", axis=0, tiled=True),
            lax.all_gather(shards[3], "fsdp", axis=0, tiled=True),
            lax.all_gather(shards[4], "fsdp", axis=0, tiled=True),
            lax.all_gather(shards[5], "fsdp", axis=0, tiled=True),
            lax.all_gather(shards[6], "fsdp", axis=0, tiled=True),
            lax.all_gather(shards[7], "fsdp", axis=0, tiled=True),
            lax.all_gather(shards[8], "fsdp", axis=0, tiled=True),
            lax.all_gather(shards[9], "fsdp", axis=0, tiled=True),
            lax.all_gather(shards[10], "fsdp", axis=0, tiled=True),
            lax.all_gather(shards[11], "fsdp", axis=0, tiled=True),
            lax.all_gather(shards[12], "fsdp", axis=0, tiled=True),
        )
        frame_rows = frames[slot]
        gain_one = whole[0].astype(jnp.float32)
        shift_one = whole[1].astype(jnp.float32)
        norm_a = layer_norm(frame_rows, gain_one, shift_one).astype(jnp.bfloat16)
        qkv = product(norm_a, whole[2])
        query = (qkv[:, :width] + whole[3].astype(jnp.float32)).astype(jnp.bfloat16)
        key = qkv[:, width : 2 * width].astype(jnp.bfloat16)
        value = (qkv[:, 2 * width :] + whole[4].astype(jnp.float32)).astype(jnp.bfloat16)
        keys_all, values_all = (
            lax.all_gather(key, "fsdp", axis=0, tiled=True),
            lax.all_gather(value, "fsdp", axis=0, tiled=True),
        )
        mixed, totals = attend(query, keys_all, values_all, valid)
        attn_in = mixed.astype(jnp.bfloat16)
        resid = frame_rows + product(attn_in, whole[5]) + whole[6].astype(jnp.float32)
        gain_two = whole[7].astype(jnp.float32)
        shift_two = whole[8].astype(jnp.float32)
        norm_f = layer_norm(resid, gain_two, shift_two).astype(jnp.bfloat16)
        upward = product(norm_f, whole[9]) + whole[10].astype(jnp.float32)
        hidden = exact_gelu(upward).astype(jnp.bfloat16)
        outputs.append(resid + product(hidden, whole[11]) + whole[12].astype(jnp.float32))
        whole = (
            lax.all_gather(shards[0], "fsdp", axis=0, tiled=True),
            lax.all_gather(shards[1], "fsdp", axis=0, tiled=True),
            lax.all_gather(shards[2], "fsdp", axis=0, tiled=True),
            lax.all_gather(shards[3], "fsdp", axis=0, tiled=True),
            lax.all_gather(shards[4], "fsdp", axis=0, tiled=True),
            lax.all_gather(shards[5], "fsdp", axis=0, tiled=True),
            lax.all_gather(shards[6], "fsdp", axis=0, tiled=True),
            lax.all_gather(shards[7], "fsdp", axis=0, tiled=True),
            lax.all_gather(shards[8], "fsdp", axis=0, tiled=True),
            lax.all_gather(shards[9], "fsdp", axis=0, tiled=True),
            lax.all_gather(shards[10], "fsdp", axis=0, tiled=True),
            lax.all_gather(shards[11], "fsdp", axis=0, tiled=True),
            lax.all_gather(shards[12], "fsdp", axis=0, tiled=True),
        )
        d_out = cotangent[slot].astype(jnp.bfloat16)
        d_hidden = product_right(d_out, whole[11])
        unused, gelu_back = jax.vjp(exact_gelu, upward)
        d_up = gelu_back(d_hidden)[0].astype(jnp.bfloat16)
        unused, norm_two_back = jax.vjp(layer_norm, resid, gain_two, shift_two)
        d_resid_norm, grad_gain_two, grad_shift_two = norm_two_back(product_right(d_up, whole[9]))
        d_resid = cotangent[slot] + d_resid_norm
        d_attn = d_resid.astype(jnp.bfloat16)
        d_mixed = product_right(d_attn, whole[5]).astype(jnp.bfloat16)
        d_query, key_terms, value_terms = attend_back(
            query, keys_all, values_all, valid, totals, d_mixed
        )
        d_key, d_value = (
            lax.psum_scatter(key_terms, "fsdp", scatter_dimension=0, tiled=True),
            lax.psum_scatter(value_terms, "fsdp", scatter_dimension=0, tiled=True),
        )
        d_query = d_query.astype(jnp.bfloat16)
        d_key = d_key.astype(jnp.bfloat16)
        d_value = d_value.astype(jnp.bfloat16)
        d_qkv = jnp.concatenate([d_query, d_key, d_value], axis=1)
        unused, norm_one_back = jax.vjp(layer_norm, frame_rows, gain_one, shift_one)
        d_frames_norm, grad_gain_one, grad_shift_one = norm_one_back(product_right(d_qkv, whole[2]))
        input_grads.append(d_resid + d_frames_norm)
        pieces = (norm_a, d_qkv, attn_in, d_attn, norm_f, d_up, hidden, d_out)
        smalls = (grad_gain_one, grad_shift_one, grad_gain_two, grad_shift_two)
        kept_pieces.append(pieces)
        small_sum = add_tuples(small_sum, smalls)
    joined = tuple(
        (jnp.concatenate([group[index] for group in kept_pieces], axis=0) for index in range(8))
    )
    owned = lax.psum_scatter(
        weight_grads(joined, small_sum), "fsdp", scatter_dimension=0, tiled=True
    )
    summed = lax.psum(
        (
            owned[0],
            owned[1],
            owned[2],
            owned[3],
            owned[4],
            owned[5],
            owned[6],
            owned[7],
            owned[8],
            owned[9],
            owned[10],
            owned[11],
            owned[12],
        ),
        "rep",
    )
    return (jnp.stack(outputs), jnp.stack(input_grads)) + tuple(summed)


LOW = jnp.bfloat16
FULL = jnp.float32
VMEM = 60 * 2**20
PACE = 1.15e9 * 1.0


def contract(left, right, left_dim, right_dim):
    return lax.dot_general(
        left, right, (((left_dim,), (right_dim,)), ((), ())), preferred_element_type=FULL
    )


def const_spec(shape):
    return pl.BlockSpec(shape, lambda *at: (0,) * len(shape), pipeline_mode=pl.Buffered(1))


def call(kernel, grid, in_specs, out_specs, out_shape, scratch=(), us=1.0, aliases=None, after=()):
    count, extra = len(in_specs), len(after)

    def body(ids, *refs):
        kernel(ids, *refs[:count], *refs[count + extra :])

    run = pl.pallas_call(
        body,
        grid_spec=pltpu.PrefetchScalarGridSpec(
            num_scalar_prefetch=1,
            grid=grid,
            in_specs=list(in_specs) + [pl.BlockSpec(memory_space=pl.ANY)] * extra,
            out_specs=out_specs,
            scratch_shapes=list(scratch),
        ),
        out_shape=out_shape,
        input_output_aliases=aliases or {},
        compiler_params=pltpu.CompilerParams(vmem_limit_bytes=VMEM),
        cost_estimate=pl.CostEstimate(flops=int(us * PACE), bytes_accessed=0, transcendentals=0),
    )
    return lambda *args: run(*args, *after)


ANYWHERE = pl.BlockSpec(memory_space=pl.ANY)


def spread(rows):
    mean = jnp.mean(rows, axis=-1, keepdims=True)
    centred = rows - mean
    scale = lax.rsqrt(jnp.mean(centred * centred, axis=-1, keepdims=True) + 1e-05)
    return centred * scale, scale


def norm_pull(unit, scale, gain, grad):
    inner = grad * gain
    along = jnp.mean(inner * unit, axis=-1, keepdims=True)
    return scale * (inner - jnp.mean(inner, axis=-1, keepdims=True) - unit * along)


def vector(ids, params_ref, at, half):
    own, far = params_ref[0:1, at : at + half], params_ref[1:2, at : at + half]
    first = ids[0] == 0
    return jnp.concatenate([jnp.where(first, own, far), jnp.where(first, far, own)], axis=1)


def struct(shape, dtype):
    return jax.ShapeDtypeStruct(shape, dtype)


def first_norm_kernel(stats, ids, frames_ref, params_ref, norm_ref):
    rows = frames_ref[0]
    width = rows.shape[1]
    half = width // 2
    mean = jnp.mean(rows, axis=-1, keepdims=True)
    centred = rows - mean
    moved = jnp.mean(centred * centred, axis=-1, keepdims=True) + 1e-05
    unit = centred * lax.rsqrt(moved)
    norm_ref[:, :width] = (unit * vector(ids, params_ref, 0, half) + vector(ids, params_ref, half, half)).astype(LOW)
    if stats:
        lane = lax.broadcasted_iota(jnp.int32, (1, 128), 1)
        out = jnp.zeros((rows.shape[0], 128), FULL)
        for at, value in enumerate((mean, jnp.sqrt(moved))):
            coarse = value.astype(LOW).astype(FULL)
            out = jnp.where(lane == 2 * at, coarse, jnp.where(lane == 2 * at + 1, value - coarse, out))
        norm_ref[:, width:] = out.astype(LOW)


def first_norm(ids, frames, params, other, after=()):
    unused, rows, width = frames.shape
    block = rows // 2
    wide = width + 128 * other
    return call(
        functools.partial(first_norm_kernel, other),
        (2,),
        [
            pl.BlockSpec((1, block, width), lambda i, ids: (ids[0] ^ other, i, 0)),
            const_spec(params.shape),
        ],
        pl.BlockSpec((block, wide), lambda i, ids: (i, 0)),
        struct((rows, wide), LOW),
        us=4,
        after=after,
    )(ids, frames, params)


def far_parts(ids, message, params_ref, half):
    width = 2 * half
    norm = message[:, :width].astype(FULL)
    stats = message[:, width:].astype(FULL)
    unit = (norm - vector(ids, params_ref, half, half)) / vector(ids, params_ref, 0, half)
    return unit, stats[:, 0:1] + stats[:, 1:2], stats[:, 2:3] + stats[:, 3:4]


def place_pieces(ids, target, base, piece_refs):
    rows = piece_refs[0].shape[-2]
    for turn in range(8):
        at = pl.multiple_of(base + ((ids[1] // 2) ^ turn) * rows, rows)
        part = piece_refs[turn // 2][turn % 2]
        target[pl.ds(at, rows), :] = part.reshape(rows, part.shape[-1])


def place_weights(ids, target, own_ref, piece_refs):
    half = own_ref.shape[0]
    target[pl.ds(pl.multiple_of(ids[0] * half, half), half), :] = own_ref[...]
    place_pieces(ids, target, (1 - ids[0]) * half, piece_refs)


def project_kernel(group, ids, own_rows, far_rows, own_ref, p0, p1, p2, p3, params_ref, out_ref, whole_ref, *refs):
    half, width = own_rows.shape
    rows_scr = refs[-1]

    @pl.when(pl.program_id(0) == 0)
    def _():
        rows_scr[0:half] = own_rows[...]
        rows_scr[half:] = far_rows[:, :width]
        if group == 0:
            refs[0][...] = rows_scr[...].T

    place_weights(ids, whole_ref, own_ref, (p0, p1, p2, p3))
    part = width // 2
    row = jnp.where(ids[0] == group, params_ref[0:1, 2 * part : 4 * part], params_ref[1:2, 2 * part : 4 * part])
    step = pl.program_id(0)
    bias = jnp.where(step == 0, row[:, :part], jnp.where(step == 2, row[:, part:], 0.0))
    out_ref[...] = (contract(rows_scr[...], whole_ref[...], 1, 0) + bias).astype(LOW)


def project(ids, group, own_rows, far_rows, own, pieces, params, after=()):
    half, width = own_rows.shape
    tile = width // 2
    piece = pl.BlockSpec((2, width // 16, tile), lambda j, ids: (0, 0, j))
    turn = group == 0
    return call(
        functools.partial(project_kernel, group),
        (3,),
        [const_spec((half, width)), const_spec(far_rows.shape)]
        + [pl.BlockSpec((width // 2, tile), lambda j, ids: (0, 2 * j + group))]
        + [piece] * 4
        + [const_spec(params.shape)],
        [pl.BlockSpec((2 * half, tile), lambda j, ids: (0, j)), pl.BlockSpec((width, tile), lambda j, ids: (0, j))]
        + [const_spec((width, 2 * half))] * turn,
        [struct((2 * half, 3 * tile), LOW), struct((width, 3 * tile), LOW)] + [struct((width, 2 * half), LOW)] * turn,
        [pltpu.VMEM((2 * half, width), LOW)],
        us=12,
        after=after,
    )(ids, own_rows, far_rows, own, *pieces, params)


def window(head, size):
    first = head * size // 128
    last = -(-(head + 1) * size // 128)
    return first * 128, last * 128, head * size - first * 128


def head_lanes(lanes, offset, size):
    lane = lax.broadcasted_iota(jnp.int32, (1, lanes), 1)
    return (lane >= offset) & (lane < offset + size)


def attend_kernel(size, per, ids, query_ref, key_ref, value_ref, bias_ref, out_ref, total_ref, acc):
    scale = size ** (-0.5)
    bias = bias_ref[...]
    lane = lax.broadcasted_iota(jnp.int32, (1, 128), 1)
    acc[...] = jnp.zeros_like(acc)
    stats = jnp.zeros((query_ref.shape[0], 128), FULL)
    for head in range(per):
        low, high, offset = window(head, size)
        inside = head_lanes(high - low, offset, size)
        query = query_ref[:, low:high]
        query = jnp.where(inside, query, jnp.zeros_like(query))
        scores = contract(query, key_ref[:, low:high], 1, 1) * scale + bias
        peak = jnp.max(scores, axis=-1, keepdims=True)
        raised = jnp.exp(scores - peak)
        summed = jnp.sum(raised, axis=-1, keepdims=True)
        probs = (raised * (1.0 / summed)).astype(LOW)
        mixed = contract(probs, value_ref[:, low:high], 1, 0)
        acc[:, low:high] += jnp.where(inside, mixed, 0.0)
        stats = jnp.where(lane == head, peak + jnp.log(summed), stats)
    out_ref[...] = acc[...].astype(LOW)
    total_ref[...] = stats.T[:per]


def attend_rows(ids, qkv, bias, after=(), tile=512, groups=2):
    rows, part = qkv.shape[0], qkv.shape[1] // 3
    per = HEADS // groups
    return call(
        functools.partial(attend_kernel, part // per, per),
        (rows // tile,),
        [
            pl.BlockSpec((tile, part), lambda i, ids: (i, 0)),
            pl.BlockSpec((rows, part), lambda i, ids: (0, 1), pipeline_mode=pl.Buffered(1)),
            pl.BlockSpec((rows, part), lambda i, ids: (0, 2), pipeline_mode=pl.Buffered(1)),
            const_spec((1, rows)),
        ],
        [
            pl.BlockSpec((tile, part), lambda i, ids: (i, 0)),
            pl.BlockSpec((per, tile), lambda i, ids: (0, i)),
        ],
        [struct((rows, part), LOW), struct((per, rows), FULL)],
        [pltpu.VMEM((tile, part), FULL)],
        us=19,
        after=after,
    )(ids, qkv, qkv, qkv, bias)


def attend_back_kernel(size, heads, ids, query_ref, key_ref, value_ref, upper_ref, bias_ref, total_ref, *refs):
    prior = refs[:-4]
    grad_ref, acc, key_sum, value_sum = refs[-4:]
    step = pl.program_id(0)
    scale = size ** (-0.5)
    bias = bias_ref[...]
    tile = query_ref.shape[0]

    @pl.when(step == 0)
    def _():
        key_sum[...] = jnp.zeros_like(key_sum)
        value_sum[...] = jnp.zeros_like(value_sum)

    acc[...] = jnp.zeros_like(acc)
    for head in heads:
        low, high, offset = window(head, size)
        inside = head_lanes(high - low, offset, size)
        query = query_ref[:, low:high]
        query = jnp.where(inside, query, jnp.zeros_like(query))
        upper = upper_ref[:, low:high]
        upper = jnp.where(inside, upper, jnp.zeros_like(upper))
        keys = key_ref[:, low:high]
        scores = contract(keys, query, 1, 1) * scale + bias
        probs = jnp.exp(scores - total_ref[head : head + 1, :])
        d_probs = contract(value_ref[:, low:high], upper, 1, 1)
        terms = probs * d_probs
        d_scores = (terms - probs * jnp.sum(terms, axis=0, keepdims=True)).astype(LOW)
        value_sum[:, low:high] += contract(probs.astype(LOW), upper, 1, 0)
        key_sum[:, low:high] += contract(d_scores, query, 1, 0)
        acc[:, low:high] += jnp.where(inside, contract(d_scores, keys, 0, 0), 0.0)
    part = acc.shape[1]
    here = pl.ds(pl.multiple_of(step * tile, tile), tile)
    grad = (acc[...] * scale).astype(LOW)
    grad_ref[here, :part] = grad + prior[0][here, :part] if prior else grad

    @pl.when(step == pl.num_programs(0) - 1)
    def _():
        key_grad, value_grad = (key_sum[...] * scale).astype(LOW), value_sum[...].astype(LOW)
        grad_ref[:, part : 2 * part] = key_grad + prior[0][:, part : 2 * part] if prior else key_grad
        grad_ref[:, 2 * part :] = value_grad + prior[0][:, 2 * part :] if prior else value_grad


def attend_back_rows(ids, group, qkv, upper, bias, totals, after, heads=None, prior=(), tile=512, groups=2):
    rows, part = qkv.shape[0], qkv.shape[1] // 3
    per = HEADS // groups
    heads = heads or range(per)
    return call(
        functools.partial(attend_back_kernel, part // per, heads),
        (rows // tile,),
        [
            pl.BlockSpec((tile, part), lambda i, ids: (i, 0)),
            pl.BlockSpec((rows, part), lambda i, ids: (0, 1), pipeline_mode=pl.Buffered(1)),
            pl.BlockSpec((rows, part), lambda i, ids: (0, 2), pipeline_mode=pl.Buffered(1)),
            pl.BlockSpec((tile, part), lambda i, ids: (i, group)),
            const_spec((rows, 1)),
            pl.BlockSpec((per, tile), lambda i, ids: (0, i)),
        ]
        + [const_spec((rows, 3 * part))] * len(prior),
        const_spec((rows, 3 * part)),
        struct((rows, 3 * part), LOW),
        [pltpu.VMEM((tile, part), FULL), pltpu.VMEM((rows, part), FULL), pltpu.VMEM((rows, part), FULL)],
        us=31 * len(heads) / per,
        after=after,
    )(ids, qkv, qkv, qkv, upper, bias, totals, *prior)


def out_kernel(ids, mixed0, mixed1, own_ref, p0, p1, p2, p3, frames_ref, far_ref, params_ref, resid_ref, norm_ref, turned_ref, whole_ref, start):
    step = pl.program_id(0)
    half = own_ref.shape[0]
    is_near = step < pl.num_programs(0) // 2

    @pl.when(step == 0)
    def _():
        place_weights(ids, whole_ref, own_ref, (p0, p1, p2, p3))

    @pl.when(is_near)
    def _():
        start[...] = frames_ref[0]

    @pl.when(jnp.logical_not(is_near))
    def _():
        unit, mean, deviation = far_parts(ids, far_ref[...], params_ref, half)
        start[...] = mean + deviation * unit

    mixed = jnp.concatenate([mixed0[...], mixed1[...]], axis=1)
    resid = start[...] + contract(mixed, whole_ref[...], 1, 0) + vector(ids, params_ref, 4 * half, half)
    resid_ref[...] = resid
    unit, unused = spread(resid)
    norm = (unit * vector(ids, params_ref, 5 * half, half) + vector(ids, params_ref, 6 * half, half)).astype(LOW)
    norm_ref[...] = norm
    turned_ref[...] = norm.T


def near_spec(tile, width, count):
    return pl.BlockSpec((1, tile, width), lambda i, ids: (ids[0], jnp.minimum(i, count // 2 - 1), 0))


def far_spec(tile, width, count):
    return pl.BlockSpec((tile, width), lambda i, ids: (jnp.maximum(i - count // 2, 0), 0))


def row_spec(tile, width):
    return pl.BlockSpec((tile, width), lambda i, ids: (i, 0))


def out_rows(ids, mixed0, mixed1, own, pieces, frames, far, params, after=(), tile=256):
    rows, part = mixed0.shape
    width = 2 * part
    count = rows // tile
    return call(
        out_kernel,
        (count,),
        [row_spec(tile, part), row_spec(tile, part), const_spec((part, width))]
        + [const_spec(array.shape) for array in pieces]
        + [near_spec(tile, width, count), far_spec(tile, far.shape[1], count), const_spec(params.shape)],
        [
            row_spec(tile, width),
            row_spec(tile, width),
            pl.BlockSpec((width, tile), lambda i, ids: (0, i)),
            const_spec((width, width)),
        ],
        [struct((rows, width), FULL), struct((rows, width), LOW), struct((width, rows), LOW), struct((width, width), LOW)],
        [pltpu.VMEM((tile, width), FULL)],
        us=12,
        after=after,
    )(ids, mixed0, mixed1, own, *pieces, frames, far, params)


def bell_parts(values):
    bell = jnp.exp(values * values * -0.5)
    return 0.5 + 0.5 * lax.erf(values * (0.5**0.5)), bell


def put_side(ids, far, refs, source):
    block = refs[0].shape[2]
    for turn in range(16):
        piece = (ids[0] ^ far) * 16 + (ids[1] ^ turn)
        rows = source[pl.ds(pl.multiple_of(piece * block, block), block), :].astype(LOW)
        if turn < 8:
            refs[0][0, turn] = rows
        else:
            refs[turn // 4 - 1][0, turn % 4] = rows


def side_shapes(rows):
    return [(1, 8, rows // 32), (1, 4, rows // 32), (1, 4, rows // 32)]


def feed_kernel(first, last, far, start, ids, norm_ref, turned_ref, *refs):
    refs = list(refs)
    take = lambda count: [refs.pop(0) for unused in range(count)]
    if first:
        cot_ref, cot_far_ref, y_in = take(3)
    else:
        dout, y_in, dn_in = take(3)
    own_ref, = take(1)
    piece_refs = take(4)
    down_refs = take(4 if far else 1)
    params_ref, = take(1)
    if start:
        take(10)
    if first:
        dout, = take(1)
    if last:
        near_out, far_out = take(2)
    else:
        y_out, = take(1)
    dn_out, = take(1)
    near_refs, far_refs = take(3), take(3)
    down_keep, down0, down1, bias_ref = take(4)
    y_acc, dn_acc, up_w, down_w, grad, grad_low, far_low, sems = refs
    step = pl.program_id(0)
    half = own_ref.shape[0]
    tile = own_ref.shape[1]
    rows = norm_ref.shape[0]
    y_copy = pltpu.make_async_copy(y_in, y_acc, sems.at[0])
    if not first:
        dn_copy = pltpu.make_async_copy(dn_in, dn_acc, sems.at[1])

    @pl.when(step == 0)
    def _():
        y_copy.start()
        if first:
            dn_acc[...] = jnp.zeros_like(dn_acc)
            dout[: rows // 2] = cot_ref[0].astype(LOW)
            dout[rows // 2 :] = cot_far_ref[...]
        else:
            dn_copy.start()

    place_weights(ids, up_w, own_ref, piece_refs)
    if far:
        place_pieces(ids, down_w, 0, down_refs)
        down = down_w[...]
    else:
        down = down_refs[0][...]
    up = up_w[...]
    upper = dout[...]
    at = pl.multiple_of(8 * half + (step + start) * tile, tile)
    raised = contract(norm_ref[...], up, 1, 0) + params_ref[far : far + 1, pl.ds(at, tile)]
    d_hidden = contract(upper, down, 1, 1)
    lower, bell = bell_parts(raised)
    hidden = (raised * lower).astype(LOW)
    d_up = (d_hidden * (lower + raised * bell * (0.5 / jnp.pi) ** 0.5)).astype(LOW)
    bias_ref[...] = jnp.sum(d_up.astype(FULL), axis=0, keepdims=True)

    @pl.when(step == 0)
    def _():
        y_copy.wait()
        if first:
            y_acc[...] += vector(ids, params_ref, 7 * half, half)
        else:
            dn_copy.wait()

    y_acc[...] += contract(hidden, down, 1, 0)
    dn_acc[...] += contract(d_up, up, 1, 1)
    end = step == pl.num_programs(0) - 1
    copies = [pltpu.make_async_copy(dn_acc, dn_out, sems.at[1])]
    if last:
        copies.append(pltpu.make_async_copy(y_acc.at[: rows // 2], near_out.at[ids[0]], sems.at[0]))
        copies.append(pltpu.make_async_copy(far_low, far_out, sems.at[2]))
    else:
        copies.append(pltpu.make_async_copy(y_acc, y_out, sems.at[0]))

    @pl.when(end)
    def _():
        if last:
            far_low[...] = y_acc[rows // 2 :].astype(LOW)
        for copy in copies:
            copy.start()

    grad[...] = contract(turned_ref[...], d_up, 1, 0)
    put_side(ids, 0, near_refs, grad)
    put_side(ids, 1, far_refs, grad)
    grad_low[...] = contract(hidden, upper, 0, 0)
    count, block = down_keep.shape[0], down_keep.shape[1]
    for turn in range(2 * count):
        low = grad_low[pl.ds(pl.multiple_of((ids[2] ^ turn) * block, block), block), :].astype(LOW)
        if turn < count:
            down_keep[turn] = low
        elif turn < count + 4:
            down0[turn - count] = low
        else:
            down1[turn - count - 4] = low

    @pl.when(end)
    def _():
        for copy in copies:
            copy.wait()


def feed_rows(ids, far, start, count, norm, turned, carry, up, up_pieces, down, params, grads=(), last=None, after=(), tile=512):
    rows, width = norm.shape
    half = up.shape[1] // 2
    tiles = half // tile
    first = carry[0].ndim == 3
    column = lambda j, ids: (ids[0] ^ far) * tiles + start + j
    own_spec = pl.BlockSpec((width // 2, tile), lambda j, ids: (0, column(j, ids)))
    piece_spec = pl.BlockSpec((2, width // 16, tile), lambda j, ids: (0, 0, start + j))
    if far:
        down_specs = [pl.BlockSpec((2, 1, tile // 8, width), lambda j, ids: (0, start + j, 0, 0))] * 4
    else:
        down_specs = [pl.BlockSpec((tile, width), lambda j, ids: (start + j, 0))]
    if first:
        carry_specs = [
            pl.BlockSpec((1, rows // 2, width), lambda j, ids: (ids[0], 0, 0), pipeline_mode=pl.Buffered(1)),
            const_spec((rows // 2, width)),
            ANYWHERE,
        ]
        out_specs, out_shape = [const_spec((rows, width))], [struct((rows, width), LOW)]
    else:
        carry_specs = [const_spec((rows, width)), ANYWHERE, ANYWHERE]
        out_specs, out_shape = [], []
    if last is not None:
        out_specs += [ANYWHERE, ANYWHERE]
        out_shape += [struct(last, FULL), struct((rows // 2, width), LOW)]
    else:
        out_specs += [ANYWHERE]
        out_shape += [struct((rows, width), FULL)]
    in_specs = (
        [const_spec((rows, width)), const_spec((width, rows))]
        + carry_specs
        + [own_spec]
        + [piece_spec] * 4
        + down_specs
        + [const_spec(params.shape)]
        + [ANYWHERE] * len(grads)
    )
    fine = tile // 16
    sides = side_shapes(width) * 2
    out_specs += [ANYWHERE]
    out_specs += [pl.BlockSpec(shape + (tile,), lambda j, ids: (0, 0, 0, start + j)) for shape in sides]
    out_specs += [
        pl.BlockSpec((8, fine, width), lambda j, ids: (0, start + j, 0)),
        pl.BlockSpec((4, fine, width), lambda j, ids: (0, start + j, 0)),
        pl.BlockSpec((4, fine, width), lambda j, ids: (0, start + j, 0)),
        pl.BlockSpec((1, tile), lambda j, ids: (0, start + j)),
    ]
    out_shape += (
        [struct((rows, width), FULL)]
        + [struct(shape + (half,), LOW) for shape in sides]
        + [struct((8, half // 16, width), LOW)]
        + [struct((4, half // 16, width), LOW)] * 2
        + [struct((1, half), FULL)]
    )
    aliases = {1 + len(in_specs) - 10 + k: len(out_shape) - 10 + k for k in range(len(grads))}
    return call(
        functools.partial(feed_kernel, first, last is not None, far, start),
        (count,),
        in_specs,
        out_specs,
        out_shape,
        [
            pltpu.VMEM((rows, width), FULL),
            pltpu.VMEM((rows, width), FULL),
            pltpu.VMEM((width, tile), LOW),
            pltpu.VMEM((tile, width), LOW),
            pltpu.VMEM((width, tile), FULL),
            pltpu.VMEM((tile, width), FULL),
            pltpu.VMEM((rows // 2, width), LOW),
            pltpu.SemaphoreType.DMA((3,)),
        ],
        us=3 + 11.5 * count,
        aliases=aliases,
        after=after,
    )(ids, norm, turned, *carry, up, *up_pieces, *down, params, *grads)


def middle_kernel(
    ids, dn_ref, resid_ref, cot_ref, got_ref, mixed0, mixed1, whole_ref, params_ref,
    d_resid_ref, d_mixed_ref, n0, n1, n2, f0, f1, f2, small_ref, grad, sums,
):
    step = pl.program_id(0)
    count = pl.num_programs(0)
    half = params_ref.shape[1] // 12

    @pl.when(step == 0)
    def _():
        grad[...] = jnp.zeros_like(grad)
        sums[...] = jnp.zeros_like(sums)

    pick = (step < count // 2).astype(FULL)
    cot = cot_ref[0] * pick + got_ref[...].astype(FULL) * (1.0 - pick)
    d_norm = dn_ref[...]
    unit, scale = spread(resid_ref[...])
    d_resid = cot + norm_pull(unit, scale, vector(ids, params_ref, 5 * half, half), d_norm)
    d_attn = d_resid.astype(LOW)
    d_resid_ref[...] = d_resid
    d_mixed_ref[...] = contract(d_attn, whole_ref[...], 1, 1).astype(LOW)
    grad[:half] += contract(mixed0[...], d_attn, 0, 0)
    grad[half:] += contract(mixed1[...], d_attn, 0, 0)
    sums[0:1] += jnp.sum(d_attn.astype(FULL), axis=0, keepdims=True)
    sums[1:2] += jnp.sum(d_norm * unit, axis=0, keepdims=True)
    sums[2:3] += jnp.sum(d_norm, axis=0, keepdims=True)
    sums[3:4] += jnp.sum(cot.astype(LOW).astype(FULL), axis=0, keepdims=True)

    @pl.when(step == count - 1)
    def _():
        put_side(ids, 0, (n0, n1, n2), grad)
        put_side(ids, 1, (f0, f1, f2), grad)
        small_ref[...] = sums[...]


def middle_rows(ids, dn, resid, cotangent, got, mixed0, mixed1, whole, params, after=(), tile=256):
    rows, width = resid.shape
    thin = row_spec(tile, width // 2)
    count = rows // tile
    wide = row_spec(tile, width)
    sides = side_shapes(width) * 2
    return call(
        middle_kernel,
        (count,),
        [wide] * 2
        + [near_spec(tile, width, count), far_spec(tile, width, count), thin, thin, const_spec((width, width)), const_spec(params.shape)],
        [wide, wide] + [const_spec(shape + (width,)) for shape in sides] + [const_spec((8, width))],
        [
            struct((rows, width), FULL),
            struct((rows, width), LOW),
        ]
        + [struct(shape + (width,), LOW) for shape in sides]
        + [
            struct((8, width), FULL),
        ],
        [pltpu.VMEM((width, width), FULL), pltpu.VMEM((8, width), FULL)],
        us=20,
        after=after,
    )(ids, dn, resid, cotangent, got, mixed0, mixed1, whole, params)


def project_grad_kernel(ids, turned_ref, grad_ref, *refs):
    more, refs = refs[:-8], refs[-8:]
    pieces, bias_ref, grad = refs[:6], refs[6], refs[7]
    step = pl.program_id(0)

    @pl.when(step < 3)
    def _():
        d_part = grad_ref[...]
        grad[...] = contract(turned_ref[...], d_part, 1, 0)
        for far in range(2):
            put_side(ids, far, pieces[3 * far : 3 * far + 3], grad)
        bias_ref[0] = jnp.sum(d_part.astype(FULL), axis=0, keepdims=True)

    if more:

        @pl.when(step >= 3)
        def _():
            for source, target in zip(more, pieces):
                target[...] = source[...]


def project_grad(ids, turned, d_group, extra=(), after=()):
    width, rows = turned.shape
    part = d_group.shape[1] // 3
    count = 5 if len(extra) else 3
    shapes = side_shapes(width) * 2
    pieces = [pl.BlockSpec(shape + (part,), lambda j, ids: (0, 0, 0, j)) for shape in shapes]
    more = [pl.BlockSpec(shape + (part,), lambda j, ids: (0, 0, 0, jnp.maximum(j - 3, 0))) for shape in shapes]
    return call(
        project_grad_kernel,
        (count,),
        [const_spec((width, rows)), pl.BlockSpec((rows, part), lambda j, ids: (0, jnp.minimum(j, 2)))]
        + more[: len(extra)],
        pieces + [pl.BlockSpec((1, 1, part), lambda j, ids: (jnp.minimum(j, 2), 0, 0))],
        [struct(shape + (count * part,), LOW) for shape in shapes] + [struct((3, 1, part), FULL)],
        [pltpu.VMEM((width, part), FULL)],
        us=11,
        after=after,
    )(ids, turned, d_group, *extra)


def last_kernel(ids, d0_ref, d1_ref, whole0, whole1, frames_ref, far_ref, d_resid_ref, params_ref, near_out, far_out, small_ref, sums, unit_scr, scale_scr):
    step = pl.program_id(0)
    count = pl.num_programs(0)
    half = params_ref.shape[1] // 12
    is_near = step < count // 2

    @pl.when(step == 0)
    def _():
        sums[...] = jnp.zeros_like(sums)

    @pl.when(is_near)
    def _():
        unit, scale = spread(frames_ref[0])
        unit_scr[...] = unit
        scale_scr[...] = jnp.broadcast_to(scale, scale_scr.shape)

    @pl.when(jnp.logical_not(is_near))
    def _():
        unit, mean, deviation = far_parts(ids, far_ref[...], params_ref, half)
        unit_scr[...] = unit
        scale_scr[...] = jnp.broadcast_to(1.0 / deviation, scale_scr.shape)

    d_norm = contract(d0_ref[...], whole0[...], 1, 1) + contract(d1_ref[...], whole1[...], 1, 1)
    unit = unit_scr[...]
    grad = d_resid_ref[...] + norm_pull(unit, scale_scr[:, 0:1], vector(ids, params_ref, 0, half), d_norm)
    sums[0:1] += jnp.sum(d_norm * unit, axis=0, keepdims=True)
    sums[1:2] += jnp.sum(d_norm, axis=0, keepdims=True)

    @pl.when(is_near)
    def _():
        near_out[0] = grad

    @pl.when(jnp.logical_not(is_near))
    def _():
        far_out[...] = grad.astype(LOW)

    @pl.when(step == count - 1)
    def _():
        small_ref[...] = sums[...]


def last_rows(ids, d0, d1, whole0, whole1, frames, far, d_resid, params, after=(), tile=256):
    rows, width = d_resid.shape
    count = rows // tile
    return call(
        last_kernel,
        (count,),
        [
            row_spec(tile, d0.shape[1]),
            row_spec(tile, d0.shape[1]),
            const_spec(whole0.shape),
            const_spec(whole0.shape),
            near_spec(tile, width, count),
            far_spec(tile, far.shape[1], count),
            row_spec(tile, width),
            const_spec(params.shape),
        ],
        [near_spec(tile, width, count), far_spec(tile, width, count), const_spec((8, width))],
        [struct(frames.shape, FULL), struct((rows // 2, width), LOW), struct((8, width), FULL)],
        [pltpu.VMEM((8, width), FULL), pltpu.VMEM((tile, width), FULL), pltpu.VMEM((tile, 128), FULL)],
        us=22,
        after=after,
    )(ids, d0, d1, whole0, whole1, frames, far, d_resid, params)


def fill_kernel(ids, whole_ref, part_ref, out_ref):
    out_ref[0] = part_ref[...].astype(FULL)


def fill_rows(ids, whole, part, after=()):
    rows, width = part.shape
    tile = rows // 2
    return call(
        fill_kernel,
        (2,),
        [pl.BlockSpec(memory_space=pl.ANY), pl.BlockSpec((tile, width), lambda i, ids: (i, 0))],
        pl.BlockSpec((1, tile, width), lambda i, ids: (1 - ids[0], i, 0)),
        struct(whole.shape, FULL),
        us=3,
        aliases={1: 0},
        after=after,
    )(ids, whole, part)


def settle_up_kernel(ids, step, refs, turn, place, out_ref):
    half = out_ref.shape[2] // 2
    rows = refs[step][turn].astype(FULL)
    for far in range(2):
        at = pl.multiple_of((ids[0] ^ far) * half, half)
        out_ref[place, :, pl.ds(at, half)] = rows[:, far * half : (far + 1) * half]


def settle_down_kernel(ids, step, refs, turn, place, out_ref):
    tiles, unused, fine, width = out_ref.shape
    out_ref[:, place] = refs[step][turn].astype(FULL).reshape(tiles, fine, width)


def settle_qkv_kernel(ids, step, refs, turn, place, qkv_ref, out_ref):
    part = refs[4].shape[2] // 3
    for group in range(2):
        ref = refs[4 * group + step]
        for at in range(3):
            into = (2 * at + group) * part
            qkv_ref[place, :, into : into + part] = ref[turn, :, at * part : (at + 1) * part].astype(FULL)
    out_ref[place] = refs[step][turn, :, 3 * part :].astype(FULL)


def settle_kernel(which, inner, inputs, ids, *refs):
    for step in range(4):

        @pl.when(pl.program_id(0) == step)
        def _():
            for turn in range(4):
                inner(ids, step, refs[:inputs], turn, turn ^ (ids[which] % 4), *refs[inputs:])


def settle(ids, which, inner, arrays, shapes, blocks, axis=0, after=()):
    def place(s, ids, rank):
        index = [0] * rank
        index[axis] = s ^ (ids[which] // 4)
        return tuple(index)

    return call(
        functools.partial(settle_kernel, which, inner, len(arrays)),
        (4,),
        [const_spec(array.shape) for array in arrays],
        [pl.BlockSpec(block, functools.partial(place, rank=len(block))) for block in blocks],
        [struct(shape, FULL) for shape in shapes],
        us=9,
        after=after,
    )(ids, *arrays)


CORE, Y, NEAR_Z, FAR_Z = 1, 2, 4, 8


def swap(array, bit):
    return lax.ppermute(array, "rep", [(at, at ^ bit) for at in range(16)])


def cross(array):
    return lax.ppermute(array, "fsdp", [(0, 1), (1, 0)])


def fold_kernel(counts, ids, *refs):
    outs = refs[sum(counts) :]
    at = 0
    for count, out_ref in zip(counts, outs):
        total = refs[at][...].astype(FULL)
        for ref in refs[at + 1 : at + count]:
            total += ref[...].astype(FULL)
        out_ref[...] = total.astype(LOW)
        at += count


def fold(ids, *jobs, after=()):
    in_specs, arrays, out_specs, out_shape = [], [], [], []
    moved = 0
    for job in jobs:
        for array, side, first, count in job:
            sides, unused, rows, columns = array.shape
            wide = sides if side is None else 1
            base = 0 if side is None else side
            if count % 4 == 0:
                block = (wide, count // 4, rows, columns)
                spec = lambda s, ids, base=base, at=first // (count // 4): (base, at + s, 0, 0)
            elif rows % 64 == 0:
                block = (wide, count, rows // 4, columns)
                spec = lambda s, ids, base=base, at=first // count: (base, at, s, 0)
            else:
                block = (wide, count, rows, columns)
                spec = lambda s, ids, base=base, at=first // count: (base, at, 0, 0)
            in_specs.append(pl.BlockSpec(block, spec))
            arrays.append(array)
            moved += wide * count * rows * columns * 2
        if count % 4 == 0:
            out_specs.append(pl.BlockSpec(block, lambda s, ids: (0, s, 0, 0)))
        elif rows % 64 == 0:
            out_specs.append(pl.BlockSpec(block, lambda s, ids: (0, 0, s, 0)))
        else:
            out_specs.append(pl.BlockSpec(block, lambda s, ids: (0, 0, 0, 0)))
        out_shape.append(struct((wide, count, rows, columns), LOW))
        moved += wide * count * rows * columns * 2
    return call(
        functools.partial(fold_kernel, [len(job) for job in jobs]),
        (4,),
        in_specs,
        out_specs,
        out_shape,
        us=6,
        after=after,
    )(ids, *arrays)


def spread_pieces(first, second):
    return first, second, swap(first, CORE), swap(second, CORE)


def join(piece, got):
    return jnp.concatenate([piece, got], axis=0)


RING = (FAR_Z, NEAR_Z, NEAR_Z | FAR_Z)


def along_z(piece):
    return jnp.concatenate([piece] + [swap(piece, bit) for bit in RING], axis=0)


def later(value, *others):
    return lax.optimization_barrier((value,) + others)[0]


def paired_device(
    frames, cotangent, clip_lengths, clip_slots, gain_attn, shift_attn, w_qkv, bias_query, bias_value,
    w_out, bias_out, gain_ffn, shift_ffn, w_up, bias_up, w_down, bias_down,
):
    unused, rows, width = frames.shape
    half = width // 2
    eighth = half // 8
    side = lax.axis_index("fsdp")
    at = lax.axis_index("rep")

    def mine(order):
        return sum(jnp.where(at & bit != 0, 8 >> k, 0) for k, bit in enumerate(order))

    plain = (CORE, Y, NEAR_Z, FAR_Z)
    turned_order = (CORE, NEAR_Z, Y, FAR_Z)
    ids = jnp.stack([side, mine(plain), mine(turned_order), at & 1]).astype(jnp.int32)

    own_small = jnp.concatenate(
        [gain_attn, shift_attn, bias_query, bias_value, bias_out, gain_ffn, shift_ffn, bias_down, bias_up]
    )[None].astype(FULL)
    params = join(own_small, cross(own_small))

    def piece_of(weight):
        return lax.dynamic_slice_in_dim(weight, (ids[1] // 2) * eighth, eighth, axis=0)

    tile = 512
    tiles = w_down.shape[0] // tile
    ff_half = w_up.shape[1] // 2
    send_qkv = piece_of(w_qkv).reshape(eighth, 3, 2, half)
    q_a = cross(send_qkv[:, :, 0].reshape(eighth, 3 * half))[None]
    send_norm = first_norm(ids, frames, params, 1)
    slots = later(clip_slots, send_norm)
    slot = jnp.where(side == 0, slots[0], slots[1])
    numbers = jnp.arange(clip_lengths.shape[0], dtype=jnp.int32)
    span = jnp.sum(jnp.where(numbers == slot, clip_lengths, 0))
    place = jnp.arange(2 * rows, dtype=jnp.int32)
    place = jnp.where(place < rows, place + side * rows, place - rows + (1 - side) * rows)
    mask = jnp.where(place < span, 0.0, -1e30).astype(FULL)
    own_norm = first_norm(ids, frames, params, 0, (send_norm,))
    far_norm = cross(send_norm)
    q_b = cross(send_qkv[:, :, 1].reshape(eighth, 3 * half))[None]
    q_a = later(q_a, own_norm)
    q_a = join(q_a, swap(q_a, NEAR_Z))
    q_a = spread_pieces(q_a, swap(q_a, Y))
    q_b = join(q_b, swap(q_b, NEAR_Z))
    send_up = piece_of(w_up)
    send_near = lax.dynamic_slice_in_dim(send_up, (1 - side) * ff_half, ff_half, axis=1)
    send_far = lax.dynamic_slice_in_dim(send_up, side * ff_half, ff_half, axis=1)
    send_out, send_near = later(piece_of(w_out), far_norm), later(send_near, far_norm)
    qkv0, whole0, norm_turned = project(ids, 0, own_norm, far_norm, w_qkv, q_a, params, (send_out, send_near, q_b))

    send_down = lax.dynamic_index_in_dim(w_down.reshape(tiles, 8, tile // 8, width), ids[1] // 2, 1, keepdims=False)
    send_down = later(send_down, qkv0)
    q_by = later(swap(q_b, Y), qkv0)
    w_o = later(cross(send_out), qkv0)[None]
    mixed0, totals0 = attend_rows(ids, qkv0, mask[None], (q_by, w_o, send_down))

    w_o = join(w_o, later(swap(w_o, NEAR_Z), mixed0))
    w_n = later(cross(send_near), mixed0)[None]
    send_cot = lax.dynamic_index_in_dim(cotangent, 1 - side, 0, keepdims=False).astype(LOW)
    send_cot = later(send_cot, mixed0)
    qkv1, whole1 = project(ids, 1, own_norm, far_norm, w_qkv, spread_pieces(q_b, q_by), params, (w_o, w_n, send_cot))

    w_oy = later(swap(w_o, Y), qkv1)
    w_n = join(w_n, later(swap(w_n, NEAR_Z), qkv1))
    w_d = later(cross(send_down), qkv1)[None]
    mixed1, totals1 = attend_rows(ids, qkv1, mask[None], (w_oy, w_n, w_d))

    w_ny = later(swap(w_n, Y), mixed1)
    w_d = join(w_d, later(swap(w_d, NEAR_Z), mixed1))
    send_far = later(send_far, mixed1)
    resid, norm_f, norm_f_turned, whole_out = out_rows(
        ids, mixed0, mixed1, w_out, spread_pieces(w_o, w_oy), frames, far_norm, params, (w_ny, w_d, send_far)
    )

    far_cot = cross(send_cot)
    w_f = later(cross(send_far), resid)[None]
    near_up = spread_pieces(w_n, w_ny)
    dout, y, dn, *grads = feed_rows(
        ids, 0, 0, 2, norm_f, norm_f_turned, (cotangent, far_cot, resid), w_up, near_up, (w_down,), params, after=(w_f,)
    )

    w_f = join(w_f, later(swap(w_f, NEAR_Z), y))
    w_dy = later(swap(w_d, Y), y)
    y, dn, near0, near0_a, near0_b, far0, far0_a, far0_b, down0, down0_a, down0_b, bias0 = feed_rows(
        ids, 0, 2, tiles - 2, norm_f, norm_f_turned, (dout, y, dn), w_up, near_up, (w_down,), params, grads, after=(w_f, w_dy)
    )

    w_fy = later(swap(w_f, Y), y)
    far_up = spread_pieces(w_f, w_fy)
    far_down = spread_pieces(w_d, w_dy)
    y, dn, *grads = feed_rows(
        ids, 1, 0, 2, norm_f, norm_f_turned, (dout, y, dn), w_up, far_up, far_down, params
    )

    def from_core(mark, *arrays):
        return [later(swap(array, CORE), mark) for array in arrays]

    def terms(first, count, *arrays):
        return [(array, 0, first, count) for array in arrays]

    near0_ga, near0_gb, far0_ga, far0_gb = from_core(y, near0_a, near0_b, far0_a, far0_b)
    down0 = down0[None]
    down0_ga, down0_gb = from_core(y, down0_a[None], down0_b[None])
    up1_xa, up1_xb, down0_z = fold(
        ids,
        terms(0, 4, far0, far0_ga),
        terms(4, 4, far0) + terms(0, 4, far0_gb),
        terms(4, 4, down0) + terms(0, 4, down0_gb),
    )
    output, far_out, dn, near1, near1_a, near1_b, far1, far1_a, far1_b, down1, down1_a, down1_b, bias1 = feed_rows(
        ids, 1, 2, tiles - 2, norm_f, norm_f_turned, (dout, y, dn), w_up, far_up, far_down, params,
        grads, frames.shape, (up1_xa, up1_xb, down0_z),
    )

    up1_oa, up1_ob = later(cross(up1_xa), dn), later(cross(up1_xb), dn)
    down0_zg = later(swap(down0_z, NEAR_Z), dn)
    d_resid, d_mixed, *o_pieces, small_mid = middle_rows(
        ids, dn, resid, cotangent, far_cot, mixed0, mixed1, whole_out, params, (up1_oa, up1_ob, down0_zg)
    )

    near1_ga, near1_gb, far1_ga, far1_gb = from_core(d_mixed, near1_a, near1_b, far1_a, far1_b)
    down1 = down1[None]
    down1_ga, down1_gb = from_core(d_mixed, down1_a[None], down1_b[None])
    up1_y, up0_xa, up0_xb, down1_z = fold(
        ids,
        terms(4, 4, near1) + terms(0, 4, near1_gb, up1_ob),
        terms(0, 4, far1, far1_ga),
        terms(4, 4, far1) + terms(0, 4, far1_gb),
        terms(4, 4, down1) + terms(0, 4, down1_gb),
    )
    d0 = attend_back_rows(ids, 0, qkv0, d_mixed, mask[:, None], totals0, (up1_y, up0_xa, up0_xb, down1_z))

    up0_oa, up0_ob = later(cross(up0_xa), d0), later(cross(up0_xb), d0)
    up1 = [near1, near1_ga, up1_oa, later(swap(up1_y, Y), d0)]
    up0 = [near0, near0_ga, up0_oa]
    up1_z, up0_y, down_x = fold(
        ids,
        terms(2, 2, *up1),
        terms(4, 4, near0) + terms(0, 4, near0_gb, up0_ob),
        terms(0, 4, down1, down1_ga, later(swap(down1_z, NEAR_Z), d0)),
    )
    q0n, q0n_a, q0n_b, q0f, q0f_a, q0f_b, small_q0 = project_grad(
        ids, norm_turned, d0, o_pieces, (up1_z, up0_y, down_x)
    )

    far_out = later(far_out, q0n)
    d1 = attend_back_rows(ids, 1, qkv1, d_mixed, mask[:, None], totals1, (far_out,), range(4))

    q0n_ga, q0n_gb, q0f_ga, q0f_gb = from_core(d1, q0n_a, q0n_b, q0f_a, q0f_b)
    up1.append(later(swap(up1_z, NEAR_Z), d1))
    up0.append(later(swap(up0_y, Y), d1))
    q0_xa, q0_xb, up1_f, up0_z = fold(
        ids,
        terms(0, 4, q0f, q0f_ga),
        terms(4, 4, q0f) + terms(0, 4, q0f_gb),
        terms(1, 1, *up1),
        terms(2, 2, *up0),
    )
    d1 = attend_back_rows(
        ids, 1, qkv1, d_mixed, mask[:, None], totals1, (q0_xa, q0_xb, up1_f, up0_z), range(4, 8), (d1,)
    )

    down = [down0, down0_ga, down0_zg, later(cross(down_x), d1)]
    up1.append(later(swap(up1_f, FAR_Z), d1))
    up0.append(later(swap(up0_z, NEAR_Z), d1))
    down_y, up0_f, up1 = fold(ids, terms(2, 2, *down), terms(1, 1, *up0), terms(0, 1, *up1))
    q1n, q1n_a, q1n_b, q1f, q1f_a, q1f_b, small_q1 = project_grad(ids, norm_turned, d1, (), (down_y, up0_f, up1))

    q1n_ga, q1n_gb, q1f_ga, q1f_gb = from_core(q1n, q1n_a, q1n_b, q1f_a, q1f_b)
    down.append(later(swap(down_y, Y), q1n))
    up0.append(later(swap(up0_f, FAR_Z), q1n))
    q1_yn, q1_yf, down_f, up0 = fold(
        ids,
        terms(4, 4, q1n) + terms(0, 4, q1n_gb),
        terms(4, 4, q1f) + terms(0, 4, q1f_gb),
        terms(1, 1, *down),
        terms(0, 1, *up0),
    )
    up = jnp.concatenate([up0[0], up1[0]], axis=2)
    frames_grad, far_grad, small_last = last_rows(
        ids, d0, d1, whole0, whole1, frames, far_norm, d_resid, params, (q1_yn, q1_yf, down_f, up)
    )

    q1 = [q1n, q1n_ga, later(swap(q1_yn, Y), far_grad)]
    q0_oa, q0_ob = later(cross(q0_xa), far_grad), later(cross(q0_xb), far_grad)
    down.append(later(swap(down_f, FAR_Z), far_grad))
    q0 = [q0n, q0n_ga, q0_oa]
    q1_x, q0_y, down = fold(
        ids,
        terms(0, 4, q1f, q1f_ga, later(swap(q1_yf, Y), far_grad)),
        terms(4, 4, q0n) + terms(0, 4, q0n_gb, q0_ob),
        terms(0, 1, *down),
    )
    up = join(up, later(swap(up, FAR_Z), q1_x))
    down = down[0]
    output = fill_rows(ids, output, cross(far_out), (up,))

    q1.append(later(cross(q1_x), output))
    q1_z = fold(ids, *[terms(at, 1, *q1) for at in (1, 2, 3)])
    far_grad = later(far_grad, q1_z[0])
    down = join(down, later(swap(down, FAR_Z), q1_z[0]))

    q0.append(later(swap(q0_y, Y), down))
    q0_z = fold(ids, *[terms(at, 1, *q0) for at in (1, 2, 3)])
    up = join(up, later(swap(up, NEAR_Z), q0_z[0]))
    q1 = fold(ids, terms(0, 1, *q1) + terms(0, 1, *[later(swap(array, bit), up) for array, bit in zip(q1_z, RING)]))[0][0]
    down = join(down, later(swap(down, Y), q1))
    q0 = fold(ids, terms(0, 1, *q0) + terms(0, 1, *[later(swap(array, bit), down) for array, bit in zip(q0_z, RING)]))[0][0]
    q1 = later(along_z(q1), q0)
    up = spread_pieces(up, later(swap(up, Y), q1))
    q0 = later(along_z(q0), up[1])
    frames_grad = fill_rows(ids, frames_grad, cross(far_grad), (q0,))
    q1 = spread_pieces(q1, later(swap(q1, Y), frames_grad))
    ff = 2 * ff_half
    block = half // 16
    up_out, = settle(ids, 1, settle_up_kernel, list(up), [(16, block, ff)], [(4, block, ff)], after=(q1[1],))
    down = spread_pieces(down, later(swap(down, NEAR_Z), up_out))
    q0 = spread_pieces(q0, later(swap(q0, Y), down[1]))
    down_out, = settle(
        ids, 2, settle_down_kernel, list(down), [(tiles, 16, tile // 16, width)], [(tiles, 4, tile // 16, width)], 1, (q0[1],)
    )

    bias_up_sum = jnp.where(side == 0, jnp.concatenate([bias0, bias1]), jnp.concatenate([bias1, bias0]))
    query_sum = jnp.concatenate([small_q0[0], small_q1[0]], axis=0)
    value_sum = jnp.concatenate([small_q0[2], small_q1[2]], axis=0)
    vectors = [small_last[0], small_last[1], query_sum, value_sum, small_mid[0], small_mid[1], small_mid[2], small_mid[3]]
    small = jnp.concatenate([v.reshape(2, half) for v in vectors] + [bias_up_sum], axis=1)
    got = cross(lax.dynamic_slice_in_dim(small, 1 - side, 1, axis=0))
    small = lax.dynamic_slice_in_dim(small, side, 1, axis=0) + got
    for bit in plain:
        small = small + swap(small, bit)
    small = small[0]
    parts = [small[k * half : (k + 1) * half] for k in range(8)] + [small[8 * half :]]

    qkv_out, out_out = settle(
        ids, 1, settle_qkv_kernel, [*q0, *q1], [(16, block, 3 * width), (16, block, width)], [(4, block, 3 * width), (4, block, width)]
    )
    return (
        output,
        frames_grad,
        parts[0],
        parts[1],
        qkv_out.reshape(half, 3 * width),
        parts[2],
        parts[3],
        out_out.reshape(half, width),
        parts[4],
        parts[5],
        parts[6],
        up_out.reshape(half, ff),
        parts[8],
        down_out.reshape(ff_half, width),
        parts[7],
    )


def solution(mesh):
    fast = mesh.shape["fsdp"] == 2 and mesh.shape["rep"] == 16
    return jax.shard_map(
        paired_device if fast else general_device,
        mesh=mesh,
        in_specs=(
            P("rep", "fsdp", None),
            P("rep", "fsdp", None),
            P(),
            P("rep"),
            P("fsdp"),
            P("fsdp"),
            P("fsdp", None),
            P("fsdp"),
            P("fsdp"),
            P("fsdp", None),
            P("fsdp"),
            P("fsdp"),
            P("fsdp"),
            P("fsdp", None),
            P("fsdp"),
            P("fsdp", None),
            P("fsdp"),
        ),
        out_specs=(
            P("rep", "fsdp", None),
            P("rep", "fsdp", None),
            P("fsdp"),
            P("fsdp"),
            P("fsdp", None),
            P("fsdp"),
            P("fsdp"),
            P("fsdp", None),
            P("fsdp"),
            P("fsdp"),
            P("fsdp"),
            P("fsdp", None),
            P("fsdp"),
            P("fsdp", None),
            P("fsdp"),
        ),
        check_vma=False,
    )
```

```python
import functools

import jax
import jax.numpy as jnp
from jax import lax
from jax.experimental import pallas as pl
from jax.experimental.pallas import tpu as pltpu
from jax.sharding import PartitionSpec as P

HEADS = 16


def layer_norm(rows, gain, shift):
    mean = jnp.mean(rows, axis=-1, keepdims=True)
    centred = rows - mean
    spread = jnp.mean(centred * centred, axis=-1, keepdims=True)
    return centred * lax.rsqrt(spread + 1e-05) * gain + shift


def exact_gelu(values):
    return jax.nn.gelu(values, approximate=False)


def product(left, right):
    return jnp.dot(left, right, preferred_element_type=jnp.float32)


def product_left(left, right):
    return lax.dot_general(
        left, right, (((0,), (0,)), ((), ())), preferred_element_type=jnp.float32
    )


def product_right(left, right):
    return lax.dot_general(
        left, right, (((1,), (1,)), ((), ())), preferred_element_type=jnp.float32
    )


def head_blocks(query, keys, values, block):
    rows, width = query.shape
    half = width // 2
    per = HEADS // 2
    size = width // HEADS
    lower = block * half
    query_part = query[:, lower : lower + half].reshape(rows, per, size)
    key_part = keys[:, lower : lower + half].reshape(keys.shape[0], per, size)
    value_part = values[:, lower : lower + half].reshape(values.shape[0], per, size)
    return (query_part, key_part, value_part)


def masked_scores(query_part, key_part, valid, scale):
    scores = (
        jnp.einsum("qhd,khd->hqk", query_part, key_part, preferred_element_type=jnp.float32) * scale
    )
    return jnp.where(valid[None, None, :], scores, -1e30)


def attend(query, keys, values, valid):
    rows, width = query.shape
    scale = (width // HEADS) ** (-0.5)
    pieces = []
    totals = []
    for block in range(2):
        query_part, key_part, value_part = head_blocks(query, keys, values, block)
        scores = masked_scores(query_part, key_part, valid, scale)
        peak = jnp.max(scores, axis=-1, keepdims=True)
        raised = jnp.exp(scores - peak)
        summed = jnp.sum(raised, axis=-1, keepdims=True)
        probs = (raised / summed).astype(jnp.bfloat16)
        mixed = jnp.einsum("hqk,khd->qhd", probs, value_part, preferred_element_type=jnp.float32)
        pieces.append(mixed.reshape(rows, width // 2))
        totals.append(peak + jnp.log(summed))
    return (jnp.concatenate(pieces, axis=1), totals)


def attend_back(query, keys, values, valid, totals, d_mixed):
    rows, width = query.shape
    scale = (width // HEADS) ** (-0.5)
    query_grads = []
    key_grads = []
    value_grads = []
    for block in range(2):
        query_part, key_part, value_part = head_blocks(query, keys, values, block)
        upper = d_mixed[:, block * (width // 2) : (block + 1) * (width // 2)].reshape(
            query_part.shape
        )
        scores = masked_scores(query_part, key_part, valid, scale)
        probs = jnp.exp(scores - totals[block])
        d_probs = jnp.einsum("qhd,khd->hqk", upper, value_part, preferred_element_type=jnp.float32)
        centre = jnp.sum(probs * d_probs, axis=-1, keepdims=True)
        d_scores = (probs * (d_probs - centre)).astype(jnp.bfloat16)
        d_query = (
            jnp.einsum("hqk,khd->qhd", d_scores, key_part, preferred_element_type=jnp.float32)
            * scale
        )
        d_key = (
            jnp.einsum("hqk,qhd->khd", d_scores, query_part, preferred_element_type=jnp.float32)
            * scale
        )
        d_value = jnp.einsum(
            "hqk,qhd->khd", probs.astype(jnp.bfloat16), upper, preferred_element_type=jnp.float32
        )
        query_grads.append(d_query.reshape(rows, width // 2))
        key_grads.append(d_key.reshape(keys.shape[0], width // 2))
        value_grads.append(d_value.reshape(keys.shape[0], width // 2))
    return (
        jnp.concatenate(query_grads, axis=1),
        jnp.concatenate(key_grads, axis=1),
        jnp.concatenate(value_grads, axis=1),
    )


def add_tuples(first, second):
    if first is None:
        return second
    return tuple((left + right for left, right in zip(first, second)))


def weight_grads(pieces, smalls):
    norm_a, d_qkv, attn_in, d_attn, norm_f, d_up, hidden, d_out = pieces
    gain_one, shift_one, gain_two, shift_two = smalls
    width = norm_a.shape[1]
    grad_qkv = product_left(norm_a, d_qkv)
    columns = jnp.sum(d_qkv.astype(jnp.float32), axis=0)
    grad_query_bias = columns[:width]
    grad_value_bias = columns[2 * width :]
    grad_out = product_left(attn_in, d_attn)
    grad_out_bias = jnp.sum(d_attn.astype(jnp.float32), axis=0)
    grad_up = product_left(norm_f, d_up)
    grad_up_bias = jnp.sum(d_up.astype(jnp.float32), axis=0)
    grad_down = product_left(hidden, d_out)
    grad_down_bias = jnp.sum(d_out.astype(jnp.float32), axis=0)
    return (
        gain_one,
        shift_one,
        grad_qkv,
        grad_query_bias,
        grad_value_bias,
        grad_out,
        grad_out_bias,
        gain_two,
        shift_two,
        grad_up,
        grad_up_bias,
        grad_down,
        grad_down_bias,
    )


def general_device(
    frames,
    cotangent,
    clip_lengths,
    clip_slots,
    gain_attn,
    shift_attn,
    w_qkv,
    bias_query,
    bias_value,
    w_out,
    bias_out,
    gain_ffn,
    shift_ffn,
    w_up,
    bias_up,
    w_down,
    bias_down,
):
    shards = (
        gain_attn,
        shift_attn,
        w_qkv,
        bias_query,
        bias_value,
        w_out,
        bias_out,
        gain_ffn,
        shift_ffn,
        w_up,
        bias_up,
        w_down,
        bias_down,
    )
    micro, rows, width = frames.shape
    group_size = lax.axis_size("fsdp")
    length_all = rows * group_size
    positions = jnp.arange(length_all, dtype=jnp.int32)
    numbers = jnp.arange(clip_lengths.shape[0], dtype=jnp.int32)
    outputs = []
    input_grads = []
    summed = None
    kept_pieces = []
    small_sum = None
    for slot in range(micro):
        span = jnp.sum(jnp.where(numbers == clip_slots[slot], clip_lengths, 0))
        valid = positions < span
        whole = (
            lax.all_gather(shards[0], "fsdp", axis=0, tiled=True),
            lax.all_gather(shards[1], "fsdp", axis=0, tiled=True),
            lax.all_gather(shards[2], "fsdp", axis=0, tiled=True),
            lax.all_gather(shards[3], "fsdp", axis=0, tiled=True),
            lax.all_gather(shards[4], "fsdp", axis=0, tiled=True),
            lax.all_gather(shards[5], "fsdp", axis=0, tiled=True),
            lax.all_gather(shards[6], "fsdp", axis=0, tiled=True),
            lax.all_gather(shards[7], "fsdp", axis=0, tiled=True),
            lax.all_gather(shards[8], "fsdp", axis=0, tiled=True),
            lax.all_gather(shards[9], "fsdp", axis=0, tiled=True),
            lax.all_gather(shards[10], "fsdp", axis=0, tiled=True),
            lax.all_gather(shards[11], "fsdp", axis=0, tiled=True),
            lax.all_gather(shards[12], "fsdp", axis=0, tiled=True),
        )
        frame_rows = frames[slot]
        gain_one = whole[0].astype(jnp.float32)
        shift_one = whole[1].astype(jnp.float32)
        norm_a = layer_norm(frame_rows, gain_one, shift_one).astype(jnp.bfloat16)
        qkv = product(norm_a, whole[2])
        query = (qkv[:, :width] + whole[3].astype(jnp.float32)).astype(jnp.bfloat16)
        key = qkv[:, width : 2 * width].astype(jnp.bfloat16)
        value = (qkv[:, 2 * width :] + whole[4].astype(jnp.float32)).astype(jnp.bfloat16)
        keys_all, values_all = (
            lax.all_gather(key, "fsdp", axis=0, tiled=True),
            lax.all_gather(value, "fsdp", axis=0, tiled=True),
        )
        mixed, totals = attend(query, keys_all, values_all, valid)
        attn_in = mixed.astype(jnp.bfloat16)
        resid = frame_rows + product(attn_in, whole[5]) + whole[6].astype(jnp.float32)
        gain_two = whole[7].astype(jnp.float32)
        shift_two = whole[8].astype(jnp.float32)
        norm_f = layer_norm(resid, gain_two, shift_two).astype(jnp.bfloat16)
        upward = product(norm_f, whole[9]) + whole[10].astype(jnp.float32)
        hidden = exact_gelu(upward).astype(jnp.bfloat16)
        outputs.append(resid + product(hidden, whole[11]) + whole[12].astype(jnp.float32))
        whole = (
            lax.all_gather(shards[0], "fsdp", axis=0, tiled=True),
            lax.all_gather(shards[1], "fsdp", axis=0, tiled=True),
            lax.all_gather(shards[2], "fsdp", axis=0, tiled=True),
            lax.all_gather(shards[3], "fsdp", axis=0, tiled=True),
            lax.all_gather(shards[4], "fsdp", axis=0, tiled=True),
            lax.all_gather(shards[5], "fsdp", axis=0, tiled=True),
            lax.all_gather(shards[6], "fsdp", axis=0, tiled=True),
            lax.all_gather(shards[7], "fsdp", axis=0, tiled=True),
            lax.all_gather(shards[8], "fsdp", axis=0, tiled=True),
            lax.all_gather(shards[9], "fsdp", axis=0, tiled=True),
            lax.all_gather(shards[10], "fsdp", axis=0, tiled=True),
            lax.all_gather(shards[11], "fsdp", axis=0, tiled=True),
            lax.all_gather(shards[12], "fsdp", axis=0, tiled=True),
        )
        d_out = cotangent[slot].astype(jnp.bfloat16)
        d_hidden = product_right(d_out, whole[11])
        unused, gelu_back = jax.vjp(exact_gelu, upward)
        d_up = gelu_back(d_hidden)[0].astype(jnp.bfloat16)
        unused, norm_two_back = jax.vjp(layer_norm, resid, gain_two, shift_two)
        d_resid_norm, grad_gain_two, grad_shift_two = norm_two_back(product_right(d_up, whole[9]))
        d_resid = cotangent[slot] + d_resid_norm
        d_attn = d_resid.astype(jnp.bfloat16)
        d_mixed = product_right(d_attn, whole[5]).astype(jnp.bfloat16)
        d_query, key_terms, value_terms = attend_back(
            query, keys_all, values_all, valid, totals, d_mixed
        )
        d_key, d_value = (
            lax.psum_scatter(key_terms, "fsdp", scatter_dimension=0, tiled=True),
            lax.psum_scatter(value_terms, "fsdp", scatter_dimension=0, tiled=True),
        )
        d_query = d_query.astype(jnp.bfloat16)
        d_key = d_key.astype(jnp.bfloat16)
        d_value = d_value.astype(jnp.bfloat16)
        d_qkv = jnp.concatenate([d_query, d_key, d_value], axis=1)
        unused, norm_one_back = jax.vjp(layer_norm, frame_rows, gain_one, shift_one)
        d_frames_norm, grad_gain_one, grad_shift_one = norm_one_back(product_right(d_qkv, whole[2]))
        input_grads.append(d_resid + d_frames_norm)
        pieces = (norm_a, d_qkv, attn_in, d_attn, norm_f, d_up, hidden, d_out)
        smalls = (grad_gain_one, grad_shift_one, grad_gain_two, grad_shift_two)
        kept_pieces.append(pieces)
        small_sum = add_tuples(small_sum, smalls)
    joined = tuple(
        (jnp.concatenate([group[index] for group in kept_pieces], axis=0) for index in range(8))
    )
    owned = lax.psum_scatter(
        weight_grads(joined, small_sum), "fsdp", scatter_dimension=0, tiled=True
    )
    summed = lax.psum(
        (
            owned[0],
            owned[1],
            owned[2],
            owned[3],
            owned[4],
            owned[5],
            owned[6],
            owned[7],
            owned[8],
            owned[9],
            owned[10],
            owned[11],
            owned[12],
        ),
        "rep",
    )
    return (jnp.stack(outputs), jnp.stack(input_grads)) + tuple(summed)


LOW = jnp.bfloat16
FULL = jnp.float32
VMEM = 60 * 2**20
PACE = 1.15e9 * 1.0


def contract(left, right, left_dim, right_dim):
    return lax.dot_general(
        left, right, (((left_dim,), (right_dim,)), ((), ())), preferred_element_type=FULL
    )


def const_spec(shape):
    return pl.BlockSpec(shape, lambda *at: (0,) * len(shape), pipeline_mode=pl.Buffered(1))


def call(kernel, grid, in_specs, out_specs, out_shape, scratch=(), us=1.0, aliases=None, after=()):
    count, extra = len(in_specs), len(after)

    def body(ids, *refs):
        kernel(ids, *refs[:count], *refs[count + extra :])

    run = pl.pallas_call(
        body,
        grid_spec=pltpu.PrefetchScalarGridSpec(
            num_scalar_prefetch=1,
            grid=grid,
            in_specs=list(in_specs) + [pl.BlockSpec(memory_space=pl.ANY)] * extra,
            out_specs=out_specs,
            scratch_shapes=list(scratch),
        ),
        out_shape=out_shape,
        input_output_aliases=aliases or {},
        compiler_params=pltpu.CompilerParams(vmem_limit_bytes=VMEM),
        cost_estimate=pl.CostEstimate(flops=int(us * PACE), bytes_accessed=0, transcendentals=0),
    )
    return lambda *args: run(*args, *after)


ANYWHERE = pl.BlockSpec(memory_space=pl.ANY)


def spread(rows):
    mean = jnp.mean(rows, axis=-1, keepdims=True)
    centred = rows - mean
    scale = lax.rsqrt(jnp.mean(centred * centred, axis=-1, keepdims=True) + 1e-05)
    return centred * scale, scale


def norm_pull(unit, scale, gain, grad):
    inner = grad * gain
    along = jnp.mean(inner * unit, axis=-1, keepdims=True)
    return scale * (inner - jnp.mean(inner, axis=-1, keepdims=True) - unit * along)


def vector(ids, params_ref, at, half):
    own, far = params_ref[0:1, at : at + half], params_ref[1:2, at : at + half]
    first = ids[0] == 0
    return jnp.concatenate([jnp.where(first, own, far), jnp.where(first, far, own)], axis=1)


def struct(shape, dtype):
    return jax.ShapeDtypeStruct(shape, dtype)


def first_norm_kernel(stats, ids, frames_ref, params_ref, norm_ref):
    rows = frames_ref[0]
    width = rows.shape[1]
    half = width // 2
    mean = jnp.mean(rows, axis=-1, keepdims=True)
    centred = rows - mean
    moved = jnp.mean(centred * centred, axis=-1, keepdims=True) + 1e-05
    unit = centred * lax.rsqrt(moved)
    norm_ref[:, :width] = (unit * vector(ids, params_ref, 0, half) + vector(ids, params_ref, half, half)).astype(LOW)
    if stats:
        lane = lax.broadcasted_iota(jnp.int32, (1, 128), 1)
        out = jnp.zeros((rows.shape[0], 128), FULL)
        for at, value in enumerate((mean, jnp.sqrt(moved))):
            coarse = value.astype(LOW).astype(FULL)
            out = jnp.where(lane == 2 * at, coarse, jnp.where(lane == 2 * at + 1, value - coarse, out))
        norm_ref[:, width:] = out.astype(LOW)


def first_norm(ids, frames, params, other, us, after=()):
    unused, rows, width = frames.shape
    block = rows // 2
    wide = width + 128 * other
    return call(
        functools.partial(first_norm_kernel, other),
        (2,),
        [
            pl.BlockSpec((1, block, width), lambda i, ids: (ids[0] ^ other, i, 0)),
            const_spec(params.shape),
        ],
        pl.BlockSpec((block, wide), lambda i, ids: (i, 0)),
        struct((rows, wide), LOW),
        us=us,
        after=after,
    )(ids, frames, params)


def far_parts(ids, message, params_ref, half):
    width = 2 * half
    norm = message[:, :width].astype(FULL)
    stats = message[:, width:].astype(FULL)
    unit = (norm - vector(ids, params_ref, half, half)) / vector(ids, params_ref, 0, half)
    return unit, stats[:, 0:1] + stats[:, 1:2], stats[:, 2:3] + stats[:, 3:4]


def place_pieces(ids, target, base, piece_refs):
    rows = piece_refs[0].shape[-2]
    for turn in range(8):
        at = pl.multiple_of(base + ((ids[1] // 2) ^ turn) * rows, rows)
        part = piece_refs[turn // 2][turn % 2]
        target[pl.ds(at, rows), :] = part.reshape(rows, part.shape[-1])


def place_weights(ids, target, own_ref, piece_refs):
    half = own_ref.shape[0]
    target[pl.ds(pl.multiple_of(ids[0] * half, half), half), :] = own_ref[...]
    place_pieces(ids, target, (1 - ids[0]) * half, piece_refs)


def project_kernel(group, ids, own_rows, far_rows, own_ref, p0, p1, p2, p3, params_ref, out_ref, whole_ref, *refs):
    half, width = own_rows.shape
    rows_scr = refs[-1]

    @pl.when(pl.program_id(0) == 0)
    def _():
        rows_scr[0:half] = own_rows[...]
        rows_scr[half:] = far_rows[:, :width]
        if group == 0:
            refs[0][...] = rows_scr[...].T

    place_weights(ids, whole_ref, own_ref, (p0, p1, p2, p3))
    part = width // 2
    row = jnp.where(ids[0] == group, params_ref[0:1, 2 * part : 4 * part], params_ref[1:2, 2 * part : 4 * part])
    step = pl.program_id(0)
    bias = jnp.where(step == 0, row[:, :part], jnp.where(step == 2, row[:, part:], 0.0))
    out_ref[...] = (contract(rows_scr[...], whole_ref[...], 1, 0) + bias).astype(LOW)


def project(ids, group, own_rows, far_rows, own, pieces, params, after=()):
    half, width = own_rows.shape
    tile = width // 2
    piece = pl.BlockSpec((2, width // 16, tile), lambda j, ids: (0, 0, j))
    turn = group == 0
    return call(
        functools.partial(project_kernel, group),
        (3,),
        [const_spec((half, width)), const_spec(far_rows.shape)]
        + [pl.BlockSpec((width // 2, tile), lambda j, ids: (0, 2 * j + group))]
        + [piece] * 4
        + [const_spec(params.shape)],
        [pl.BlockSpec((2 * half, tile), lambda j, ids: (0, j)), pl.BlockSpec((width, tile), lambda j, ids: (0, j))]
        + [const_spec((width, 2 * half))] * turn,
        [struct((2 * half, 3 * tile), LOW), struct((width, 3 * tile), LOW)] + [struct((width, 2 * half), LOW)] * turn,
        [pltpu.VMEM((2 * half, width), LOW)],
        us=12,
        after=after,
    )(ids, own_rows, far_rows, own, *pieces, params)


def window(head, size):
    first = head * size // 128
    last = -(-(head + 1) * size // 128)
    return first * 128, last * 128, head * size - first * 128


def head_lanes(lanes, offset, size):
    lane = lax.broadcasted_iota(jnp.int32, (1, lanes), 1)
    return (lane >= offset) & (lane < offset + size)


PACE_TWO = 1.4426950408889634


def lanes(count):
    return lax.broadcasted_iota(jnp.int32, (1, count), 1)


def free_lane(offset, size):
    return 0 if offset >= 8 else offset + size


def in_three(column):
    first = column.astype(LOW)
    rest = column - first.astype(FULL)
    second = rest.astype(LOW)
    return first, second, (rest - second.astype(FULL)).astype(LOW)


def put_lanes(rows, at, columns):
    lane = lanes(rows.shape[1])
    for turn, column in enumerate(columns):
        rows = jnp.where(lane == at + turn, column, rows)
    return rows


def attend_kernel(size, per, ids, query_ref, key_ref, value_ref, bias_ref, out_ref, total_ref, acc):
    scale = size ** (-0.5)
    one = jnp.ones((1, 1), LOW)
    mask = jnp.broadcast_to(bias_ref[...], (128, bias_ref.shape[1])).T[:, 0:1].astype(LOW)
    acc[...] = jnp.zeros_like(acc)
    stats = jnp.zeros((query_ref.shape[0], 128), FULL)
    for head in range(per):
        low, high, offset = window(head, size)
        inside = head_lanes(high - low, offset, size)
        free = free_lane(offset, size)
        query = query_ref[:, low:high]
        query = put_lanes(jnp.where(inside, query, jnp.zeros_like(query)), free, (one,))
        scores = contract(query, put_lanes(key_ref[:, low:high], free, (mask,)), 1, 1)
        peak = jnp.max(scores, axis=-1, keepdims=True)
        raised = jnp.exp2((scores - peak) * (scale * PACE_TWO))
        summed = jnp.sum(raised, axis=-1, keepdims=True)
        mixed = contract(raised.astype(LOW), value_ref[:, low:high], 1, 0) * (1.0 / summed)
        acc[:, low:high] += jnp.where(inside, mixed, 0.0)
        stats = jnp.where(lanes(128) == head, peak * scale + jnp.log(summed), stats)
    out_ref[...] = acc[...].astype(LOW)
    total_ref[...] = stats.T[:per]


def attend_rows(ids, qkv, bias, after=(), tile=512, groups=2):
    rows, part = qkv.shape[0], qkv.shape[1] // 3
    per = HEADS // groups
    return call(
        functools.partial(attend_kernel, part // per, per),
        (rows // tile,),
        [
            pl.BlockSpec((tile, part), lambda i, ids: (i, 0)),
            pl.BlockSpec((rows, part), lambda i, ids: (0, 1), pipeline_mode=pl.Buffered(1)),
            pl.BlockSpec((rows, part), lambda i, ids: (0, 2), pipeline_mode=pl.Buffered(1)),
            const_spec((1, rows)),
        ],
        [
            pl.BlockSpec((tile, part), lambda i, ids: (i, 0)),
            pl.BlockSpec((per, tile), lambda i, ids: (0, i)),
        ],
        [struct((rows, part), LOW), struct((per, rows), FULL)],
        [pltpu.VMEM((tile, part), FULL)],
        us=19,
        after=after,
    )(ids, qkv, qkv, qkv, bias)


def attend_back_kernel(size, heads, ids, query_ref, key_ref, value_ref, upper_ref, bias_ref, total_ref, *refs):
    prior = refs[:-4]
    grad_ref, acc, key_sum, value_sum = refs[-4:]
    step = pl.program_id(0)
    scale = size ** (-0.5)
    bias = bias_ref[...]
    tile = query_ref.shape[0]

    @pl.when(step == 0)
    def _():
        key_sum[...] = jnp.zeros_like(key_sum)
        value_sum[...] = jnp.zeros_like(value_sum)

    acc[...] = jnp.zeros_like(acc)
    for head in heads:
        low, high, offset = window(head, size)
        inside = head_lanes(high - low, offset, size)
        query = query_ref[:, low:high]
        query = jnp.where(inside, query, jnp.zeros_like(query))
        upper = upper_ref[:, low:high]
        upper = jnp.where(inside, upper, jnp.zeros_like(upper))
        keys = key_ref[:, low:high]
        scores = contract(keys, query, 1, 1) * scale + bias
        probs = jnp.exp(scores - total_ref[head : head + 1, :])
        d_probs = contract(value_ref[:, low:high], upper, 1, 1)
        terms = probs * d_probs
        d_scores = (terms - probs * jnp.sum(terms, axis=0, keepdims=True)).astype(LOW)
        value_sum[:, low:high] += contract(probs.astype(LOW), upper, 1, 0)
        key_sum[:, low:high] += contract(d_scores, query, 1, 0)
        acc[:, low:high] += jnp.where(inside, contract(d_scores, keys, 0, 0), 0.0)
    part = acc.shape[1]
    here = pl.ds(pl.multiple_of(step * tile, tile), tile)
    grad = (acc[...] * scale).astype(LOW)
    grad_ref[here, :part] = grad + prior[0][here, :part] if prior else grad

    @pl.when(step == pl.num_programs(0) - 1)
    def _():
        key_grad, value_grad = (key_sum[...] * scale).astype(LOW), value_sum[...].astype(LOW)
        grad_ref[:, part : 2 * part] = key_grad + prior[0][:, part : 2 * part] if prior else key_grad
        grad_ref[:, 2 * part :] = value_grad + prior[0][:, 2 * part :] if prior else value_grad


def attend_back_rows(ids, group, qkv, upper, bias, totals, after, heads=None, prior=(), tile=512, groups=2):
    rows, part = qkv.shape[0], qkv.shape[1] // 3
    per = HEADS // groups
    heads = heads or range(per)
    return call(
        functools.partial(attend_back_kernel, part // per, heads),
        (rows // tile,),
        [
            pl.BlockSpec((tile, part), lambda i, ids: (i, 0)),
            pl.BlockSpec((rows, part), lambda i, ids: (0, 1), pipeline_mode=pl.Buffered(1)),
            pl.BlockSpec((rows, part), lambda i, ids: (0, 2), pipeline_mode=pl.Buffered(1)),
            pl.BlockSpec((tile, part), lambda i, ids: (i, group)),
            const_spec((rows, 1)),
            pl.BlockSpec((per, tile), lambda i, ids: (0, i)),
        ]
        + [const_spec((rows, 3 * part))] * len(prior),
        const_spec((rows, 3 * part)),
        struct((rows, 3 * part), LOW),
        [pltpu.VMEM((tile, part), FULL), pltpu.VMEM((rows, part), FULL), pltpu.VMEM((rows, part), FULL)],
        us=31 * len(heads) / per,
        after=after,
    )(ids, qkv, qkv, qkv, upper, bias, totals, *prior)


def out_kernel(ids, mixed0, mixed1, own_ref, p0, p1, p2, p3, frames_ref, far_ref, params_ref, resid_ref, norm_ref, turned_ref, whole_ref, start):
    step = pl.program_id(0)
    half = own_ref.shape[0]
    is_near = step < pl.num_programs(0) // 2

    @pl.when(step == 0)
    def _():
        place_weights(ids, whole_ref, own_ref, (p0, p1, p2, p3))

    @pl.when(is_near)
    def _():
        start[...] = frames_ref[0]

    @pl.when(jnp.logical_not(is_near))
    def _():
        unit, mean, deviation = far_parts(ids, far_ref[...], params_ref, half)
        start[...] = mean + deviation * unit

    mixed = jnp.concatenate([mixed0[...], mixed1[...]], axis=1)
    resid = start[...] + contract(mixed, whole_ref[...], 1, 0) + vector(ids, params_ref, 4 * half, half)
    resid_ref[...] = resid
    unit, unused = spread(resid)
    norm = (unit * vector(ids, params_ref, 5 * half, half) + vector(ids, params_ref, 6 * half, half)).astype(LOW)
    norm_ref[...] = norm
    turned_ref[...] = norm.T


def near_spec(tile, width, count):
    return pl.BlockSpec((1, tile, width), lambda i, ids: (ids[0], jnp.minimum(i, count // 2 - 1), 0))


def far_spec(tile, width, count):
    return pl.BlockSpec((tile, width), lambda i, ids: (jnp.maximum(i - count // 2, 0), 0))


def row_spec(tile, width):
    return pl.BlockSpec((tile, width), lambda i, ids: (i, 0))


def out_rows(ids, mixed0, mixed1, own, pieces, frames, far, params, after=(), tile=256):
    rows, part = mixed0.shape
    width = 2 * part
    count = rows // tile
    return call(
        out_kernel,
        (count,),
        [row_spec(tile, part), row_spec(tile, part), const_spec((part, width))]
        + [const_spec(array.shape) for array in pieces]
        + [near_spec(tile, width, count), far_spec(tile, far.shape[1], count), const_spec(params.shape)],
        [
            row_spec(tile, width),
            row_spec(tile, width),
            pl.BlockSpec((width, tile), lambda i, ids: (0, i)),
            const_spec((width, width)),
        ],
        [struct((rows, width), FULL), struct((rows, width), LOW), struct((width, rows), LOW), struct((width, width), LOW)],
        [pltpu.VMEM((tile, width), FULL)],
        us=12,
        after=after,
    )(ids, mixed0, mixed1, own, *pieces, frames, far, params)


def bell_parts(values):
    bell = jnp.exp(values * values * -0.5)
    return 0.5 + 0.5 * lax.erf(values * (0.5**0.5)), bell


def put_side(ids, far, refs, source):
    block = refs[0].shape[2]
    for turn in range(16):
        piece = (ids[0] ^ far) * 16 + (ids[1] ^ turn)
        rows = source[pl.ds(pl.multiple_of(piece * block, block), block), :].astype(LOW)
        if turn < 8:
            refs[0][0, turn] = rows
        else:
            refs[turn // 4 - 1][0, turn % 4] = rows


def side_shapes(rows):
    return [(1, 8, rows // 32), (1, 4, rows // 32), (1, 4, rows // 32)]


def feed_kernel(first, last, far, start, ids, norm_ref, turned_ref, *refs):
    refs = list(refs)
    take = lambda count: [refs.pop(0) for unused in range(count)]
    if first:
        cot_ref, cot_far_ref, y_in = take(3)
    else:
        dout, y_in, dn_in = take(3)
    own_ref, = take(1)
    piece_refs = take(4)
    down_refs = take(4 if far else 1)
    params_ref, = take(1)
    if start:
        take(10)
    if first:
        dout, = take(1)
    if last:
        near_out, far_out = take(2)
    else:
        y_out, = take(1)
    dn_out, = take(1)
    near_refs, far_refs = take(3), take(3)
    down_keep, down0, down1, bias_ref = take(4)
    y_acc, dn_acc, up_w, down_w, grad, grad_low, far_low, sems = refs
    step = pl.program_id(0)
    half = own_ref.shape[0]
    tile = own_ref.shape[1]
    rows = norm_ref.shape[0]
    y_copy = pltpu.make_async_copy(y_in, y_acc, sems.at[0])
    if not first:
        dn_copy = pltpu.make_async_copy(dn_in, dn_acc, sems.at[1])

    @pl.when(step == 0)
    def _():
        y_copy.start()
        if first:
            dn_acc[...] = jnp.zeros_like(dn_acc)
            dout[: rows // 2] = cot_ref[0].astype(LOW)
            dout[rows // 2 :] = cot_far_ref[...]
        else:
            dn_copy.start()

    place_weights(ids, up_w, own_ref, piece_refs)
    if far:
        place_pieces(ids, down_w, 0, down_refs)
        down = down_w[...]
    else:
        down = down_refs[0][...]
    up = up_w[...]
    upper = dout[...]
    at = pl.multiple_of(8 * half + (step + start) * tile, tile)
    raised = contract(norm_ref[...], up, 1, 0) + params_ref[far : far + 1, pl.ds(at, tile)]
    d_hidden = contract(upper, down, 1, 1)
    lower, bell = bell_parts(raised)
    hidden = (raised * lower).astype(LOW)
    d_up = (d_hidden * (lower + raised * bell * (0.5 / jnp.pi) ** 0.5)).astype(LOW)
    bias_ref[...] = jnp.sum(d_up.astype(FULL), axis=0, keepdims=True)

    @pl.when(step == 0)
    def _():
        y_copy.wait()
        if first:
            y_acc[...] += vector(ids, params_ref, 7 * half, half)
        else:
            dn_copy.wait()

    y_acc[...] += contract(hidden, down, 1, 0)
    dn_acc[...] += contract(d_up, up, 1, 1)
    end = step == pl.num_programs(0) - 1
    copies = [pltpu.make_async_copy(dn_acc, dn_out, sems.at[1])]
    if last:
        copies.append(pltpu.make_async_copy(y_acc.at[: rows // 2], near_out.at[ids[0]], sems.at[0]))
        copies.append(pltpu.make_async_copy(far_low, far_out, sems.at[2]))
    else:
        copies.append(pltpu.make_async_copy(y_acc, y_out, sems.at[0]))

    @pl.when(end)
    def _():
        if last:
            far_low[...] = y_acc[rows // 2 :].astype(LOW)
        for copy in copies:
            copy.start()

    grad[...] = contract(turned_ref[...], d_up, 1, 0)
    put_side(ids, 0, near_refs, grad)
    put_side(ids, 1, far_refs, grad)
    grad_low[...] = contract(hidden, upper, 0, 0)
    count, block = down_keep.shape[0], down_keep.shape[1]
    for turn in range(2 * count):
        low = grad_low[pl.ds(pl.multiple_of((ids[2] ^ turn) * block, block), block), :].astype(LOW)
        if turn < count:
            down_keep[turn] = low
        elif turn < count + 4:
            down0[turn - count] = low
        else:
            down1[turn - count - 4] = low

    @pl.when(end)
    def _():
        for copy in copies:
            copy.wait()


def feed_rows(ids, far, start, count, norm, turned, carry, up, up_pieces, down, params, grads=(), last=None, after=(), tile=512):
    rows, width = norm.shape
    half = up.shape[1] // 2
    tiles = half // tile
    first = carry[0].ndim == 3
    column = lambda j, ids: (ids[0] ^ far) * tiles + start + j
    own_spec = pl.BlockSpec((width // 2, tile), lambda j, ids: (0, column(j, ids)))
    piece_spec = pl.BlockSpec((2, width // 16, tile), lambda j, ids: (0, 0, start + j))
    if far:
        down_specs = [pl.BlockSpec((2, 1, tile // 8, width), lambda j, ids: (0, start + j, 0, 0))] * 4
    else:
        down_specs = [pl.BlockSpec((tile, width), lambda j, ids: (start + j, 0))]
    if first:
        carry_specs = [
            pl.BlockSpec((1, rows // 2, width), lambda j, ids: (ids[0], 0, 0), pipeline_mode=pl.Buffered(1)),
            const_spec((rows // 2, width)),
            ANYWHERE,
        ]
        out_specs, out_shape = [const_spec((rows, width))], [struct((rows, width), LOW)]
    else:
        carry_specs = [const_spec((rows, width)), ANYWHERE, ANYWHERE]
        out_specs, out_shape = [], []
    if last is not None:
        out_specs += [ANYWHERE, ANYWHERE]
        out_shape += [struct(last, FULL), struct((rows // 2, width), LOW)]
    else:
        out_specs += [ANYWHERE]
        out_shape += [struct((rows, width), FULL)]
    in_specs = (
        [const_spec((rows, width)), const_spec((width, rows))]
        + carry_specs
        + [own_spec]
        + [piece_spec] * 4
        + down_specs
        + [const_spec(params.shape)]
        + [ANYWHERE] * len(grads)
    )
    fine = tile // 16
    sides = side_shapes(width) * 2
    out_specs += [ANYWHERE]
    out_specs += [pl.BlockSpec(shape + (tile,), lambda j, ids: (0, 0, 0, start + j)) for shape in sides]
    out_specs += [
        pl.BlockSpec((8, fine, width), lambda j, ids: (0, start + j, 0)),
        pl.BlockSpec((4, fine, width), lambda j, ids: (0, start + j, 0)),
        pl.BlockSpec((4, fine, width), lambda j, ids: (0, start + j, 0)),
        pl.BlockSpec((1, tile), lambda j, ids: (0, start + j)),
    ]
    out_shape += (
        [struct((rows, width), FULL)]
        + [struct(shape + (half,), LOW) for shape in sides]
        + [struct((8, half // 16, width), LOW)]
        + [struct((4, half // 16, width), LOW)] * 2
        + [struct((1, half), FULL)]
    )
    aliases = {1 + len(in_specs) - 10 + k: len(out_shape) - 10 + k for k in range(len(grads))}
    return call(
        functools.partial(feed_kernel, first, last is not None, far, start),
        (count,),
        in_specs,
        out_specs,
        out_shape,
        [
            pltpu.VMEM((rows, width), FULL),
            pltpu.VMEM((rows, width), FULL),
            pltpu.VMEM((width, tile), LOW),
            pltpu.VMEM((tile, width), LOW),
            pltpu.VMEM((width, tile), FULL),
            pltpu.VMEM((tile, width), FULL),
            pltpu.VMEM((rows // 2, width), LOW),
            pltpu.SemaphoreType.DMA((3,)),
        ],
        us=3 + 11.5 * count,
        aliases=aliases,
        after=after,
    )(ids, norm, turned, *carry, up, *up_pieces, *down, params, *grads)


def middle_kernel(
    ids, dn_ref, resid_ref, cot_ref, got_ref, mixed0, mixed1, whole_ref, params_ref,
    d_resid_ref, d_mixed_ref, n0, n1, n2, f0, f1, f2, small_ref, grad, sums,
):
    step = pl.program_id(0)
    count = pl.num_programs(0)
    half = params_ref.shape[1] // 12

    @pl.when(step == 0)
    def _():
        grad[...] = jnp.zeros_like(grad)
        sums[...] = jnp.zeros_like(sums)

    pick = (step < count // 2).astype(FULL)
    cot = cot_ref[0] * pick + got_ref[...].astype(FULL) * (1.0 - pick)
    d_norm = dn_ref[...]
    unit, scale = spread(resid_ref[...])
    d_resid = cot + norm_pull(unit, scale, vector(ids, params_ref, 5 * half, half), d_norm)
    d_attn = d_resid.astype(LOW)
    d_resid_ref[...] = d_resid
    d_mixed_ref[...] = contract(d_attn, whole_ref[...], 1, 1).astype(LOW)
    grad[:half] += contract(mixed0[...], d_attn, 0, 0)
    grad[half:] += contract(mixed1[...], d_attn, 0, 0)
    sums[0:1] += jnp.sum(d_attn.astype(FULL), axis=0, keepdims=True)
    sums[1:2] += jnp.sum(d_norm * unit, axis=0, keepdims=True)
    sums[2:3] += jnp.sum(d_norm, axis=0, keepdims=True)
    sums[3:4] += jnp.sum(cot.astype(LOW).astype(FULL), axis=0, keepdims=True)

    @pl.when(step == count - 1)
    def _():
        put_side(ids, 0, (n0, n1, n2), grad)
        put_side(ids, 1, (f0, f1, f2), grad)
        small_ref[...] = sums[...]


def middle_rows(ids, dn, resid, cotangent, got, mixed0, mixed1, whole, params, after=(), tile=256):
    rows, width = resid.shape
    thin = row_spec(tile, width // 2)
    count = rows // tile
    wide = row_spec(tile, width)
    sides = side_shapes(width) * 2
    return call(
        middle_kernel,
        (count,),
        [wide] * 2
        + [near_spec(tile, width, count), far_spec(tile, width, count), thin, thin, const_spec((width, width)), const_spec(params.shape)],
        [wide, wide] + [const_spec(shape + (width,)) for shape in sides] + [const_spec((8, width))],
        [
            struct((rows, width), FULL),
            struct((rows, width), LOW),
        ]
        + [struct(shape + (width,), LOW) for shape in sides]
        + [
            struct((8, width), FULL),
        ],
        [pltpu.VMEM((width, width), FULL), pltpu.VMEM((8, width), FULL)],
        us=20,
        after=after,
    )(ids, dn, resid, cotangent, got, mixed0, mixed1, whole, params)


def project_grad_kernel(ids, turned_ref, grad_ref, *refs):
    more, refs = refs[:-8], refs[-8:]
    pieces, bias_ref, grad = refs[:6], refs[6], refs[7]
    step = pl.program_id(0)

    @pl.when(step < 3)
    def _():
        d_part = grad_ref[...]
        grad[...] = contract(turned_ref[...], d_part, 1, 0)
        for far in range(2):
            put_side(ids, far, pieces[3 * far : 3 * far + 3], grad)
        bias_ref[0] = jnp.sum(d_part.astype(FULL), axis=0, keepdims=True)

    if more:

        @pl.when(step >= 3)
        def _():
            for source, target in zip(more, pieces):
                target[...] = source[...]


def project_grad(ids, turned, d_group, extra=(), after=()):
    width, rows = turned.shape
    part = d_group.shape[1] // 3
    count = 5 if len(extra) else 3
    shapes = side_shapes(width) * 2
    pieces = [pl.BlockSpec(shape + (part,), lambda j, ids: (0, 0, 0, j)) for shape in shapes]
    more = [pl.BlockSpec(shape + (part,), lambda j, ids: (0, 0, 0, jnp.maximum(j - 3, 0))) for shape in shapes]
    return call(
        project_grad_kernel,
        (count,),
        [const_spec((width, rows)), pl.BlockSpec((rows, part), lambda j, ids: (0, jnp.minimum(j, 2)))]
        + more[: len(extra)],
        pieces + [pl.BlockSpec((1, 1, part), lambda j, ids: (jnp.minimum(j, 2), 0, 0))],
        [struct(shape + (count * part,), LOW) for shape in shapes] + [struct((3, 1, part), FULL)],
        [pltpu.VMEM((width, part), FULL)],
        us=11,
        after=after,
    )(ids, turned, d_group, *extra)


def last_kernel(ids, d0_ref, d1_ref, whole0, whole1, frames_ref, far_ref, d_resid_ref, params_ref, near_out, far_out, small_ref, sums, unit_scr, scale_scr):
    step = pl.program_id(0)
    count = pl.num_programs(0)
    half = params_ref.shape[1] // 12
    is_near = step < count // 2

    @pl.when(step == 0)
    def _():
        sums[...] = jnp.zeros_like(sums)

    @pl.when(is_near)
    def _():
        unit, scale = spread(frames_ref[0])
        unit_scr[...] = unit
        scale_scr[...] = jnp.broadcast_to(scale, scale_scr.shape)

    @pl.when(jnp.logical_not(is_near))
    def _():
        unit, mean, deviation = far_parts(ids, far_ref[...], params_ref, half)
        unit_scr[...] = unit
        scale_scr[...] = jnp.broadcast_to(1.0 / deviation, scale_scr.shape)

    d_norm = contract(d0_ref[...], whole0[...], 1, 1) + contract(d1_ref[...], whole1[...], 1, 1)
    unit = unit_scr[...]
    grad = d_resid_ref[...] + norm_pull(unit, scale_scr[:, 0:1], vector(ids, params_ref, 0, half), d_norm)
    sums[0:1] += jnp.sum(d_norm * unit, axis=0, keepdims=True)
    sums[1:2] += jnp.sum(d_norm, axis=0, keepdims=True)

    @pl.when(is_near)
    def _():
        near_out[0] = grad

    @pl.when(jnp.logical_not(is_near))
    def _():
        far_out[...] = grad.astype(LOW)

    @pl.when(step == count - 1)
    def _():
        small_ref[...] = sums[...]


def last_rows(ids, d0, d1, whole0, whole1, frames, far, d_resid, params, after=(), tile=256):
    rows, width = d_resid.shape
    count = rows // tile
    return call(
        last_kernel,
        (count,),
        [
            row_spec(tile, d0.shape[1]),
            row_spec(tile, d0.shape[1]),
            const_spec(whole0.shape),
            const_spec(whole0.shape),
            near_spec(tile, width, count),
            far_spec(tile, far.shape[1], count),
            row_spec(tile, width),
            const_spec(params.shape),
        ],
        [near_spec(tile, width, count), far_spec(tile, width, count), const_spec((8, width))],
        [struct(frames.shape, FULL), struct((rows // 2, width), LOW), struct((8, width), FULL)],
        [pltpu.VMEM((8, width), FULL), pltpu.VMEM((tile, width), FULL), pltpu.VMEM((tile, 128), FULL)],
        us=22,
        after=after,
    )(ids, d0, d1, whole0, whole1, frames, far, d_resid, params)


def fill_kernel(ids, whole_ref, part_ref, out_ref):
    out_ref[0] = part_ref[...].astype(FULL)


def fill_rows(ids, whole, part, after=()):
    rows, width = part.shape
    tile = rows // 2
    return call(
        fill_kernel,
        (2,),
        [pl.BlockSpec(memory_space=pl.ANY), pl.BlockSpec((tile, width), lambda i, ids: (i, 0))],
        pl.BlockSpec((1, tile, width), lambda i, ids: (1 - ids[0], i, 0)),
        struct(whole.shape, FULL),
        us=0.1,
        aliases={1: 0},
        after=after,
    )(ids, whole, part)


def settle_up_kernel(ids, step, refs, turn, place, out_ref):
    half = out_ref.shape[2] // 2
    for far in range(2):
        at = pl.multiple_of((ids[0] ^ far) * half, half)
        out_ref[place, :, pl.ds(at, half)] = refs[4 * far + step][turn].astype(FULL)


def settle_down_kernel(ids, step, refs, turn, place, out_ref):
    tiles, unused, fine, width = out_ref.shape
    out_ref[:, place] = refs[step][turn].astype(FULL).reshape(tiles, fine, width)


def settle_qkv_kernel(ids, step, refs, turn, place, qkv_ref, out_ref):
    part = refs[4].shape[2] // 3
    for group in range(2):
        ref = refs[4 * group + step]
        for at in range(3):
            into = (2 * at + group) * part
            qkv_ref[place, :, into : into + part] = ref[turn, :, at * part : (at + 1) * part].astype(FULL)
    out_ref[place] = refs[step][turn, :, 3 * part :].astype(FULL)


def settle_kernel(which, inner, inputs, ids, *refs):
    for step in range(4):

        @pl.when(pl.program_id(0) == step)
        def _():
            for turn in range(4):
                inner(ids, step, refs[:inputs], turn, turn ^ (ids[which] % 4), *refs[inputs:])


def settle(ids, which, inner, arrays, shapes, blocks, axis=0, after=()):
    def place(s, ids, rank):
        index = [0] * rank
        index[axis] = s ^ (ids[which] // 4)
        return tuple(index)

    return call(
        functools.partial(settle_kernel, which, inner, len(arrays)),
        (4,),
        [const_spec(array.shape) for array in arrays],
        [pl.BlockSpec(block, functools.partial(place, rank=len(block))) for block in blocks],
        [struct(shape, FULL) for shape in shapes],
        us=0.1,
        after=after,
    )(ids, *arrays)


CORE, Y, NEAR_Z, FAR_Z = 1, 2, 4, 8


def swap(array, bit):
    return lax.ppermute(array, "rep", [(at, at ^ bit) for at in range(16)])


def cross(array):
    return lax.ppermute(array, "fsdp", [(0, 1), (1, 0)])


def fold_kernel(jobs, ids, *refs):
    outs = refs[sum(map(sum, jobs)) :]
    at = 0
    for job, out_ref in zip(jobs, outs):
        for place, count in enumerate(job):
            total = refs[at][0].astype(FULL)
            for ref in refs[at + 1 : at + count]:
                total += ref[0].astype(FULL)
            out_ref[place] = total.astype(LOW)
            at += count


def fold(ids, *jobs, us=6, after=()):
    in_specs, arrays, out_specs, out_shape, counts = [], [], [], [], []
    for job in jobs:
        job = job if isinstance(job, tuple) else (job,)
        for terms in job:
            for array, side, first, count in terms:
                unused, unused, rows, columns = array.shape
                if count % 4 == 0:
                    block = (1, count // 4, rows, columns)
                    spec = lambda s, ids, side=side, at=first // (count // 4): (side, at + s, 0, 0)
                else:
                    block = (1, count, rows, columns)
                    spec = lambda s, ids, side=side, at=first // count: (side, at, 0, 0)
                in_specs.append(pl.BlockSpec(block, spec))
                arrays.append(array)
        counts.append([len(terms) for terms in job])
        moving = count % 4 == 0
        out_specs.append(pl.BlockSpec((len(job),) + block[1:], lambda s, ids, moving=moving: (0, s * moving, 0, 0)))
        out_shape.append(struct((len(job), count, rows, columns), LOW))
    return call(
        functools.partial(fold_kernel, counts),
        (4,),
        in_specs,
        out_specs,
        out_shape,
        us=us,
        after=after,
    )(ids, *arrays)


def spread_pieces(first, second):
    return first, second, swap(first, CORE), swap(second, CORE)


def join(piece, got):
    return jnp.concatenate([piece, got], axis=0)


RING = (FAR_Z, NEAR_Z, NEAR_Z | FAR_Z)


def along_z(piece):
    return jnp.concatenate([piece] + [swap(piece, bit) for bit in RING], axis=0)


def later(value, *others):
    return lax.optimization_barrier((value,) + others)[0]


def paired_device(
    frames, cotangent, clip_lengths, clip_slots, gain_attn, shift_attn, w_qkv, bias_query, bias_value,
    w_out, bias_out, gain_ffn, shift_ffn, w_up, bias_up, w_down, bias_down,
):
    unused, rows, width = frames.shape
    half = width // 2
    eighth = half // 8
    side = lax.axis_index("fsdp")
    at = lax.axis_index("rep")

    def mine(order):
        return sum(jnp.where(at & bit != 0, 8 >> k, 0) for k, bit in enumerate(order))

    plain = (CORE, Y, NEAR_Z, FAR_Z)
    turned_order = (CORE, NEAR_Z, Y, FAR_Z)
    ids = jnp.stack([side, mine(plain), mine(turned_order), at & 1]).astype(jnp.int32)

    own_small = jnp.concatenate(
        [gain_attn, shift_attn, bias_query, bias_value, bias_out, gain_ffn, shift_ffn, bias_down, bias_up]
    )[None].astype(FULL)
    params = join(own_small, cross(own_small))

    eighth_at = later((ids[1] // 2) * eighth, own_small)

    def piece_of(weight):
        return lax.dynamic_slice_in_dim(weight, eighth_at, eighth, axis=0)

    tile = 512
    tiles = w_down.shape[0] // tile
    ff_half = w_up.shape[1] // 2
    send_qkv = piece_of(w_qkv).reshape(eighth, 3, 2, half)
    q_a = cross(send_qkv[:, :, 0].reshape(eighth, 3 * half))[None]
    send_norm = first_norm(ids, frames, params, 1, 4)
    slots = later(clip_slots, send_norm)
    slot = jnp.where(side == 0, slots[0], slots[1])
    numbers = jnp.arange(clip_lengths.shape[0], dtype=jnp.int32)
    span = jnp.sum(jnp.where(numbers == slot, clip_lengths, 0))
    place = jnp.arange(2 * rows, dtype=jnp.int32)
    place = jnp.where(place < rows, place + side * rows, place - rows + (1 - side) * rows)
    mask = jnp.where(place < span, 0.0, -1e30).astype(FULL)
    own_norm = first_norm(ids, frames, params, 0, 20, (send_norm,))
    far_norm = cross(send_norm)
    q_b = cross(send_qkv[:, :, 1].reshape(eighth, 3 * half))[None]
    q_a = later(q_a, own_norm)
    q_a = join(q_a, swap(q_a, NEAR_Z))
    q_a = spread_pieces(q_a, swap(q_a, Y))
    q_b = join(q_b, swap(q_b, NEAR_Z))
    send_up = piece_of(w_up)
    send_near = lax.dynamic_slice_in_dim(send_up, (1 - side) * ff_half, ff_half, axis=1)
    send_far = lax.dynamic_slice_in_dim(send_up, side * ff_half, ff_half, axis=1)
    send_out, send_near = later(piece_of(w_out), far_norm), later(send_near, far_norm)
    qkv0, whole0, norm_turned = project(ids, 0, own_norm, far_norm, w_qkv, q_a, params, (send_out, send_near, q_b))

    send_down = lax.dynamic_index_in_dim(w_down.reshape(tiles, 8, tile // 8, width), ids[1] // 2, 1, keepdims=False)
    send_down = later(send_down, qkv0)
    q_by = later(swap(q_b, Y), qkv0)
    w_o = later(cross(send_out), qkv0)[None]
    mixed0, totals0 = attend_rows(ids, qkv0, mask[None], (q_by, w_o, send_down))

    w_o = join(w_o, later(swap(w_o, NEAR_Z), mixed0))
    w_n = later(cross(send_near), mixed0)[None]
    send_cot = lax.dynamic_index_in_dim(cotangent, 1 - side, 0, keepdims=False).astype(LOW)
    send_cot = later(send_cot, mixed0)
    qkv1, whole1 = project(ids, 1, own_norm, far_norm, w_qkv, spread_pieces(q_b, q_by), params, (w_o, w_n, send_cot))

    w_oy = later(swap(w_o, Y), qkv1)
    w_n = join(w_n, later(swap(w_n, NEAR_Z), qkv1))
    w_d = later(cross(send_down), qkv1)[None]
    mixed1, totals1 = attend_rows(ids, qkv1, mask[None], (w_oy, w_n, w_d))

    w_ny = later(swap(w_n, Y), mixed1)
    w_d = join(w_d, later(swap(w_d, NEAR_Z), mixed1))
    send_far = later(send_far, mixed1)
    resid, norm_f, norm_f_turned, whole_out = out_rows(
        ids, mixed0, mixed1, w_out, spread_pieces(w_o, w_oy), frames, far_norm, params, (w_ny, w_d, send_far)
    )

    far_cot = cross(send_cot)
    w_f = later(cross(send_far), resid)[None]
    near_up = spread_pieces(w_n, w_ny)
    dout, y, dn, *grads = feed_rows(
        ids, 0, 0, 2, norm_f, norm_f_turned, (cotangent, far_cot, resid), w_up, near_up, (w_down,), params, after=(w_f,)
    )

    w_f = join(w_f, later(swap(w_f, NEAR_Z), y))
    w_dy = later(swap(w_d, Y), y)
    y, dn, near0, near0_a, near0_b, far0, far0_a, far0_b, down0, down0_a, down0_b, bias0 = feed_rows(
        ids, 0, 2, tiles - 2, norm_f, norm_f_turned, (dout, y, dn), w_up, near_up, (w_down,), params, grads, after=(w_f, w_dy)
    )

    w_fy = later(swap(w_f, Y), y)
    far_up = spread_pieces(w_f, w_fy)
    far_down = spread_pieces(w_d, w_dy)
    y, dn, *grads = feed_rows(
        ids, 1, 0, 2, norm_f, norm_f_turned, (dout, y, dn), w_up, far_up, far_down, params
    )

    def from_core(mark, *arrays):
        return [later(swap(array, CORE), mark) for array in arrays]

    def terms(first, count, *arrays):
        return [(array, 0, first, count) for array in arrays]

    near0_ga, near0_gb, far0_ga, far0_gb = from_core(y, near0_a, near0_b, far0_a, far0_b)
    down0 = down0[None]
    down0_ga, down0_gb = from_core(y, down0_a[None], down0_b[None])
    up1_x, down0_z = fold(
        ids,
        (terms(0, 4, far0, far0_ga), terms(4, 4, far0) + terms(0, 4, far0_gb)),
        terms(4, 4, down0) + terms(0, 4, down0_gb),
    )
    output, far_out, dn, near1, near1_a, near1_b, far1, far1_a, far1_b, down1, down1_a, down1_b, bias1 = feed_rows(
        ids, 1, 2, tiles - 2, norm_f, norm_f_turned, (dout, y, dn), w_up, far_up, far_down, params,
        grads, frames.shape, (up1_x, down0_z),
    )

    def second(array):
        return [(array, 1, 0, 4)]

    up1_o = later(cross(up1_x), dn)
    down0_zg = later(swap(down0_z, NEAR_Z), dn)
    d_resid, d_mixed, *o_pieces, small_mid = middle_rows(
        ids, dn, resid, cotangent, far_cot, mixed0, mixed1, whole_out, params, (up1_o, down0_zg)
    )

    near1_ga, near1_gb, far1_ga, far1_gb = from_core(d_mixed, near1_a, near1_b, far1_a, far1_b)
    down1 = down1[None]
    down1_ga, down1_gb = from_core(d_mixed, down1_a[None], down1_b[None])
    up1_y, up0_x, down1_z = fold(
        ids,
        terms(4, 4, near1) + terms(0, 4, near1_gb) + second(up1_o),
        (terms(0, 4, far1, far1_ga), terms(4, 4, far1) + terms(0, 4, far1_gb)),
        terms(4, 4, down1) + terms(0, 4, down1_gb),
    )
    d0 = attend_back_rows(ids, 0, qkv0, d_mixed, mask[:, None], totals0, (up1_y, up0_x, down1_z))

    up0_o = later(cross(up0_x), d0)
    up1 = [near1, near1_ga, up1_o, later(swap(up1_y, Y), d0)]
    up0 = [near0, near0_ga, up0_o]
    up1_z, up0_y, down_x = fold(
        ids,
        terms(2, 2, *up1),
        terms(4, 4, near0) + terms(0, 4, near0_gb) + second(up0_o),
        terms(0, 4, down1, down1_ga, later(swap(down1_z, NEAR_Z), d0)),
    )
    q0n, q0n_a, q0n_b, q0f, q0f_a, q0f_b, small_q0 = project_grad(
        ids, norm_turned, d0, o_pieces, (up1_z, up0_y, down_x)
    )

    d1 = attend_back_rows(ids, 1, qkv1, d_mixed, mask[:, None], totals1, (q0n,), range(4))

    q0n_ga, q0n_gb, q0f_ga, q0f_gb = from_core(d1, q0n_a, q0n_b, q0f_a, q0f_b)
    up1.append(later(swap(up1_z, NEAR_Z), d1))
    up0.append(later(swap(up0_y, Y), d1))
    down = [down0, down0_ga, down0_zg, later(cross(down_x), d1)]
    q0_xa, q0_xb, up1_f, up0_z, down_y = fold(
        ids,
        terms(4, 4, q0f) + terms(0, 4, q0f_gb),
        terms(0, 4, q0f, q0f_ga),
        terms(1, 1, *up1),
        terms(2, 2, *up0),
        terms(2, 2, *down),
    )
    d1 = attend_back_rows(
        ids, 1, qkv1, d_mixed, mask[:, None], totals1, (q0_xa, q0_xb, up1_f, up0_z, down_y), range(4, 8), (d1,)
    )

    up1.append(later(swap(up1_f, FAR_Z), d1))
    up0.append(later(swap(up0_z, NEAR_Z), d1))
    down.append(later(swap(down_y, Y), d1))
    up1, up0_f, down_f = fold(ids, terms(0, 1, *up1), terms(1, 1, *up0), terms(1, 1, *down))
    up1 = up1[0]
    q0_oa = later(cross(q0_xa), d1)
    q1n, q1n_a, q1n_b, q1f, q1f_a, q1f_b, small_q1 = project_grad(
        ids, norm_turned, d1, (), (down_f, up0_f, up1, q0_oa)
    )

    q1n_ga, q1n_gb, q1f_ga, q1f_gb = from_core(q1n, q1n_a, q1n_b, q1f_a, q1f_b)
    q0_ob = later(cross(q0_xb), q1n)
    q0 = [q0n, q0n_ga, q0_ob]
    q1_x, q0_y = fold(
        ids,
        (terms(0, 4, q1f, q1f_ga), terms(4, 4, q1f) + terms(0, 4, q1f_gb)),
        terms(4, 4, q0n) + terms(0, 4, q0n_gb, q0_oa),
    )
    far_out = later(far_out, q1_x)
    frames_grad, far_grad, small_last = last_rows(
        ids, d0, d1, whole0, whole1, frames, far_norm, d_resid, params, (q1_x, q0_y)
    )

    q1_o = later(cross(q1_x), far_grad)
    q1 = [q1n, q1n_ga, q1_o]
    q0.append(later(swap(q0_y, Y), far_grad))
    up0.append(later(swap(up0_f, FAR_Z), far_grad))
    down.append(later(swap(down_f, FAR_Z), far_grad))
    q1_y, *q0_z, down, up0 = fold(
        ids,
        terms(4, 4, q1n) + terms(0, 4, q1n_gb) + second(q1_o),
        *[terms(at, 1, *q0) for at in (1, 2, 3)],
        terms(0, 1, *down),
        terms(0, 1, *up0),
    )
    down, up0 = down[0], up0[0]
    up1 = join(up1, later(swap(up1, FAR_Z), q1_y))
    small_last = later(small_last, q1_y)
    bias_up_sum = jnp.where(side == 0, jnp.concatenate([bias0, bias1]), jnp.concatenate([bias1, bias0]))
    query_sum = jnp.concatenate([small_q0[0], small_q1[0]], axis=0)
    value_sum = jnp.concatenate([small_q0[2], small_q1[2]], axis=0)
    vectors = [small_last[0], small_last[1], query_sum, value_sum, small_mid[0], small_mid[1], small_mid[2], small_mid[3]]
    small = jnp.concatenate([v.reshape(2, half) for v in vectors] + [bias_up_sum], axis=1)
    small_far = cross(lax.dynamic_slice_in_dim(small, 1 - side, 1, axis=0))
    small = lax.dynamic_slice_in_dim(small, side, 1, axis=0)

    q1.append(later(swap(q1_y, Y), up1))
    q1_z = fold(ids, *[terms(at, 1, *q1) for at in (1, 2, 3)], us=0.1)
    far_grad = later(far_grad, q1_z[0])
    down = join(down, later(swap(down, FAR_Z), q1_z[0]))
    up0 = join(up0, later(swap(up0, FAR_Z), q1_z[0]))
    up1 = join(up1, later(swap(up1, NEAR_Z), q1_z[0]))
    small = small + later(small_far, q1_z[0])
    output = fill_rows(ids, output, cross(far_out), (down, up0, up1, small))
    small = small + later(swap(small, CORE), output)

    q0_got = [later(swap(array, bit), output) for array, bit in zip(q0_z, RING)]
    q0 = fold(ids, terms(0, 1, *q0) + terms(0, 1, *q0_got), us=0.1, after=(small,))[0][0]
    q1_got = [later(swap(array, bit), q0) for array, bit in zip(q1_z, RING)]
    q1 = fold(ids, terms(0, 1, *q1) + terms(0, 1, *q1_got), us=0.1)[0][0]
    down = join(down, later(swap(down, Y), q1))
    up0 = join(up0, later(swap(up0, NEAR_Z), q1))
    up1 = spread_pieces(up1, later(swap(up1, Y), q1))
    frames_grad = fill_rows(ids, frames_grad, cross(far_grad), (down, up0))
    small = small + later(swap(small, Y), frames_grad)
    q0 = later(along_z(q0), frames_grad)
    q1 = later(along_z(q1), q0)
    up0 = spread_pieces(up0, later(swap(up0, Y), q1))
    ff = 2 * ff_half
    block = half // 16
    up_out, = settle(ids, 1, settle_up_kernel, [*up0, *up1], [(16, block, ff)], [(4, block, ff)], after=(small,))
    small = small + later(swap(small, NEAR_Z), up_out)
    q0 = spread_pieces(q0, later(swap(q0, Y), up_out))
    q1 = spread_pieces(q1, later(swap(q1, Y), up_out))
    down = spread_pieces(down, later(swap(down, NEAR_Z), q1[1]))
    down_out, = settle(
        ids, 2, settle_down_kernel, list(down), [(tiles, 16, tile // 16, width)], [(tiles, 4, tile // 16, width)], 1, (q0[1], small)
    )
    small = small + later(swap(small, FAR_Z), down_out)

    small = small[0]
    parts = [small[k * half : (k + 1) * half] for k in range(8)] + [small[8 * half :]]

    qkv_out, out_out = settle(
        ids, 1, settle_qkv_kernel, [*q0, *q1], [(16, block, 3 * width), (16, block, width)], [(4, block, 3 * width), (4, block, width)]
    )
    return (
        output,
        frames_grad,
        parts[0],
        parts[1],
        qkv_out.reshape(half, 3 * width),
        parts[2],
        parts[3],
        out_out.reshape(half, width),
        parts[4],
        parts[5],
        parts[6],
        up_out.reshape(half, ff),
        parts[8],
        down_out.reshape(ff_half, width),
        parts[7],
    )


def solution(mesh):
    fast = mesh.shape["fsdp"] == 2 and mesh.shape["rep"] == 16
    return jax.shard_map(
        paired_device if fast else general_device,
        mesh=mesh,
        in_specs=(
            P("rep", "fsdp", None),
            P("rep", "fsdp", None),
            P(),
            P("rep"),
            P("fsdp"),
            P("fsdp"),
            P("fsdp", None),
            P("fsdp"),
            P("fsdp"),
            P("fsdp", None),
            P("fsdp"),
            P("fsdp"),
            P("fsdp"),
            P("fsdp", None),
            P("fsdp"),
            P("fsdp", None),
            P("fsdp"),
        ),
        out_specs=(
            P("rep", "fsdp", None),
            P("rep", "fsdp", None),
            P("fsdp"),
            P("fsdp"),
            P("fsdp", None),
            P("fsdp"),
            P("fsdp"),
            P("fsdp", None),
            P("fsdp"),
            P("fsdp"),
            P("fsdp"),
            P("fsdp", None),
            P("fsdp"),
            P("fsdp", None),
            P("fsdp"),
        ),
        check_vma=False,
    )
```
